128 devices in a mesh: replica: 8 (over x, core), tensor: 16 (over z, y).
Axes of the slice: x: 4, y: 4, z: 4, core: 2. Of those that a mesh axis runs over, the one named last changes fastest.
Arguments:
- gradient: bfloat16 [8, 2, 768, 4096], P(None, None, 'tensor', 'replica'), may hold values from -110 to 110
- momentum: float32 [8, 2, 768, 4096], P(None, None, 'tensor', 'replica'), may hold values from -110 to 110
Outputs:
- update: bfloat16 [8, 2, 768, 4096], P(None, None, 'tensor')
- new_momentum: float32 [8, 2, 768, 4096], P(None, None, 'tensor', 'replica')
The draws below stay inside these ranges and needn't reach their ends.
All inputs are finite; a program needn't handle non-finite values.
Results may differ from the reference program's by a relative error of at most 0.019.
Values may be sent and summed in bfloat16 or wider, within the bound.
No kernel may reach another device: no remote copies, remote signals or barrier semaphores. Data moves between devices by JAX's collectives and lax.ppermute only.
A program may use at most 128 MiB of HBM per device.

```python
import math
import jax
import jax.numpy as jnp
from jax import lax

D = 4096
FF = 768
CHOSEN = 8
ITERS = 2


def scaled_entries(key, noise, high_scale):
    first_key, second_key = jax.random.split(key)
    shape = noise.shape
    row_scale = jnp.exp(jax.random.uniform(first_key, shape[:-1] + (1,), jnp.float32, 0.0, math.log(high_scale)))
    col_scale = jnp.exp(jax.random.uniform(second_key, shape[:-2] + (1, shape[-1]), jnp.float32, 0.0, math.log(high_scale)))
    return 0.1 * noise * row_scale * col_scale


def draw_gradient(key, part):
    key = jax.random.fold_in(key, 11)
    noise_key, scale_key = jax.random.split(key, 2)
    shape = (CHOSEN, 2, FF, D)
    noise = jnp.clip(jax.random.normal(noise_key, shape, jnp.float32), -4.0, 4.0)
    values = scaled_entries(scale_key, noise, 10.0)
    return values.astype(jnp.bfloat16)


def draw_momentum(key, part):
    key = jax.random.fold_in(key, 23)
    noise_key, scale_key = jax.random.split(key, 2)
    shape = (CHOSEN, 2, FF, D)
    noise = jnp.clip(jax.random.normal(noise_key, shape, jnp.float32), -4.0, 4.0)
    values = scaled_entries(scale_key, noise, 10.0)
    return values.astype(jnp.float32)


def setup_inputs(seed: int = 0) -> dict:
    key_of = jax.random.split(jax.random.key(seed), 3)
    return {
        "gradient": draw_gradient(jax.random.fold_in(key_of[2], 71), 0),
        "momentum": draw_momentum(jax.random.fold_in(key_of[2], 71), 0),
    }


momentum_decay = 0.95
coef_linear = 3.4445
coef_gram = -4.775
coef_square = 2.0315
epsilon = 1e-07

def orthogonalize(matrix):
    norm_value = jnp.sqrt(jnp.sum(jnp.square(matrix.astype(jnp.float32))))
    iterate = (matrix.astype(jnp.float32) / (norm_value + epsilon)).astype(jnp.bfloat16)
    for repeat in range(ITERS):
        gram_matrix = jnp.dot(iterate, iterate.T, preferred_element_type=jnp.float32).astype(jnp.bfloat16)
        square_term = jnp.dot(gram_matrix, gram_matrix, preferred_element_type=jnp.float32)
        poly_term = (coef_gram * gram_matrix.astype(jnp.float32) + coef_square * square_term).astype(jnp.bfloat16)
        product = jnp.dot(poly_term, iterate, preferred_element_type=jnp.float32)
        iterate = (coef_linear * iterate.astype(jnp.float32) + product).astype(jnp.bfloat16)
    scale_factor = 0.2 * math.sqrt(max(FF, D))
    return (scale_factor * iterate.astype(jnp.float32)).astype(jnp.bfloat16)

def reference(gradient, momentum):
    new_momentum = momentum_decay * momentum + gradient.astype(jnp.float32)
    look_ahead = (gradient.astype(jnp.float32) + momentum_decay * new_momentum).astype(jnp.bfloat16)
    matrices = look_ahead.reshape(2 * CHOSEN, FF, D)
    update = lax.map(orthogonalize, matrices).reshape(CHOSEN, 2, FF, D)
    return (update, new_momentum)
```

```python
import functools
import math

import jax
import jax.numpy as jnp
from jax import lax
from jax.experimental import pallas as pl
from jax.experimental.pallas import tpu as pltpu
from jax.sharding import PartitionSpec as P

D = 4096
FF = 768

momentum_decay = 0.95
coef_linear = 3.4445
coef_gram = -4.775
coef_square = 2.0315
epsilon = 1e-07
scale_factor = 0.2 * math.sqrt(max(FF, D))

BLOCK = 256
HALF = FF
VMEM = pl.BlockSpec(memory_space=pltpu.VMEM)
PARAMS = pltpu.CompilerParams(vmem_limit_bytes=48 * 1024 * 1024)
F32, BF16 = jnp.float32, jnp.bfloat16


def replica_place():
    index = lax.axis_index("replica")
    return index // 2, index % 2


def shift(value, steps, cross=0):
    pairs = [
        (chip * 2 + core, ((chip + steps) % 4) * 2 + (core ^ cross))
        for chip in range(4)
        for core in range(2)
    ]
    return lax.ppermute(value, "replica", pairs)


def dot_t(left, right):
    return lax.dot_general(left, right, (((1,), (1,)), ((), ())), preferred_element_type=F32)


def dot(left, right):
    return jnp.dot(left, right, preferred_element_type=F32)


def gram_kernel(rows_ref, keep_ref, send_ref):
    core = lax.axis_index("replica") % 2

    def rows(index):
        return rows_ref[pl.ds(index * BLOCK, BLOCK), :]

    halves = (((0, 0), (1, 0), (1, 1)), ((2, 0), (2, 1), (2, 2)))
    for mine in range(2):

        @pl.when(core == mine)
        def _():
            for place in range(3):
                kept, sent = halves[mine][place], halves[1 - mine][place]
                where = pl.ds(place * BLOCK, BLOCK)
                keep_ref[where, :] = dot_t(rows(kept[0]), rows(kept[1]))
                send_ref[where, :] = dot_t(rows(sent[0]), rows(sent[1])).astype(BF16)


def partial_gram(rows):
    return pl.pallas_call(
        gram_kernel,
        out_shape=(
            jax.ShapeDtypeStruct((HALF, BLOCK), F32),
            jax.ShapeDtypeStruct((HALF, BLOCK), BF16),
        ),
        in_specs=[VMEM],
        out_specs=(VMEM, VMEM),
        compiler_params=PARAMS,
    )(rows)


PIECE = HALF // 4


def chip_sum_kernel(keep_ref, got_ref, own_ref, next_ref, last_ref, far_ref):
    chip = lax.axis_index("replica") // 2

    def total(steps):
        where = pl.ds(pl.multiple_of(((chip + steps) % 4) * PIECE, PIECE), PIECE)
        return keep_ref[where, :] + got_ref[where, :].astype(F32)

    own_ref[...] = total(0)
    next_ref[...] = total(1).astype(BF16)
    last_ref[...] = total(3).astype(BF16)
    far_ref[...] = total(2).astype(BF16)


def chip_sum(keep, got):
    return pl.pallas_call(
        chip_sum_kernel,
        out_shape=(jax.ShapeDtypeStruct((PIECE, BLOCK), F32),)
        + (jax.ShapeDtypeStruct((PIECE, BLOCK), BF16),) * 3,
        in_specs=[VMEM, VMEM],
        out_specs=(VMEM,) * 4,
        compiler_params=PARAMS,
    )(keep, got)


def ring_sum_kernel(own_ref, a_ref, b_ref, c_ref, out_ref):
    total = own_ref[...] + a_ref[...].astype(F32) + b_ref[...].astype(F32) + c_ref[...].astype(F32)
    out_ref[...] = total.astype(BF16)


def ring_sum(own, first, second, third):
    return pl.pallas_call(
        ring_sum_kernel,
        out_shape=jax.ShapeDtypeStruct((PIECE, BLOCK), BF16),
        in_specs=[VMEM] * 4,
        out_specs=VMEM,
        compiler_params=PARAMS,
    )(own, first, second, third)


def chain_kernel(*refs):
    pieces, rows_ref, out_ref, packed, gram = refs[:8], refs[8], refs[9], refs[10], refs[11]
    index = lax.axis_index("replica")
    chip, core = index // 2, index % 2
    for steps in range(4):
        start = pl.multiple_of(((chip + steps) % 4) * PIECE, PIECE)
        packed[core, pl.ds(start, PIECE), :] = pieces[steps][...]
        packed[1 - core, pl.ds(start, PIECE), :] = pieces[4 + steps][...]
    row_id = lax.broadcasted_iota(jnp.int32, (BLOCK, BLOCK), 0)
    col_id = lax.broadcasted_iota(jnp.int32, (BLOCK, BLOCK), 1)
    diagonal = row_id == col_id
    places = ((0, 0), (1, 0), (1, 1), (2, 0), (2, 1), (2, 2))
    blocks = [packed[place // 3, pl.ds((place % 3) * BLOCK, BLOCK), :] for place in range(6)]
    squares = sum(
        jnp.sum(jnp.where(diagonal, block.astype(F32), 0.0))
        for block, (row, col) in zip(blocks, places)
        if row == col
    )
    squares = jnp.full((1, 1), squares, F32)
    scale = 1.0 / (jnp.sqrt(squares) + epsilon)
    for block, (row, col) in zip(blocks, places):
        scaled = (block.astype(F32) * scale) * scale
        gram[pl.ds(row * BLOCK, BLOCK), pl.ds(col * BLOCK, BLOCK)] = scaled.astype(BF16)
        if row != col:
            gram[pl.ds(col * BLOCK, BLOCK), pl.ds(row * BLOCK, BLOCK)] = scaled.T.astype(BF16)

    gram_0 = gram[...]
    poly_0 = (coef_gram * gram_0.astype(F32) + coef_square * dot(gram_0, gram_0)).astype(BF16)
    half_way = (coef_linear * gram_0.astype(F32) + dot(poly_0, gram_0)).astype(BF16)
    gram_1 = (coef_linear * half_way.astype(F32) + dot(half_way, poly_0)).astype(BF16)
    poly_1 = (coef_gram * gram_1.astype(F32) + coef_square * dot(gram_1, gram_1)).astype(BF16)
    rows = rows_ref[...]
    first = ((coef_linear * rows.astype(F32) + dot(poly_0, rows)) * scale).astype(BF16)
    second = coef_linear * first.astype(F32) + dot(poly_1, first)
    out_ref[...] = (scale_factor * second).astype(BF16)


def chain(pieces, rows):
    return pl.pallas_call(
        chain_kernel,
        out_shape=jax.ShapeDtypeStruct(rows.shape, BF16),
        in_specs=[VMEM] * 9,
        out_specs=VMEM,
        scratch_shapes=[pltpu.VMEM((2, HALF, BLOCK), BF16), pltpu.VMEM((FF, FF), BF16)],
        compiler_params=PARAMS,
    )(*pieces, rows)


def local(gradient, momentum):
    new_momentum = momentum_decay * momentum + gradient.astype(F32)
    look_ahead = (gradient.astype(F32) + momentum_decay * new_momentum).astype(BF16)
    experts, pairs, row_count, col_count = look_ahead.shape
    flat_rows = look_ahead.reshape(experts * pairs, row_count, col_count)
    rows = lax.all_to_all(flat_rows, "tensor", split_axis=0, concat_axis=0, tiled=True)
    rows = rows.reshape(FF, col_count)

    keep, send = partial_gram(rows)
    own, to_next, to_last, to_far = chip_sum(keep, shift(send, 0, 1))
    mine = ring_sum(own, shift(to_next, 1), shift(to_last, -1), shift(to_far, 2))
    here = (mine, shift(mine, -1), shift(mine, 2), shift(mine, 1))
    other = tuple(shift(piece, 0, 1) for piece in here)
    finished = chain(here + other, rows)

    finished = finished.reshape(experts * pairs, row_count, col_count)
    back = lax.all_to_all(finished, "tensor", split_axis=0, concat_axis=0, tiled=True)
    whole = lax.all_gather(back.reshape(FF, col_count), "replica", axis=1, tiled=True)
    update = whole.reshape(experts, pairs, row_count, whole.shape[1])
    return (update, new_momentum)


def solution(mesh):
    in_specs = (P(None, None, "tensor", "replica"), P(None, None, "tensor", "replica"))
    out_specs = (P(None, None, "tensor", None), P(None, None, "tensor", "replica"))
    return jax.shard_map(local, mesh=mesh, in_specs=in_specs, out_specs=out_specs, check_vma=False)
```

```python
import functools
import math

import jax
import jax.numpy as jnp
from jax import lax
from jax.experimental import pallas as pl
from jax.experimental.pallas import tpu as pltpu
from jax.sharding import PartitionSpec as P

D = 4096
FF = 768

momentum_decay = 0.95
coef_linear = 3.4445
coef_gram = -4.775
coef_square = 2.0315
epsilon = 1e-07
scale_factor = 0.2 * math.sqrt(max(FF, D))

WIDTH = 512
EARLY = 128
LATE = WIDTH - EARLY
BLOCK = 256
HALF = FF
VMEM = pl.BlockSpec(memory_space=pltpu.VMEM)
PARAMS = pltpu.CompilerParams(vmem_limit_bytes=48 * 1024 * 1024)
F32, BF16 = jnp.float32, jnp.bfloat16


def replica_place():
    index = lax.axis_index("replica")
    return index // 2, index % 2


def shift(value, steps, cross=0):
    pairs = [
        (chip * 2 + core, ((chip + steps) % 4) * 2 + (core ^ cross))
        for chip in range(4)
        for core in range(2)
    ]
    return lax.ppermute(value, "replica", pairs)


def dot_t(left, right):
    return lax.dot_general(left, right, (((1,), (1,)), ((), ())), preferred_element_type=F32)


def dot(left, right):
    return jnp.dot(left, right, preferred_element_type=F32)


def gram_kernel(rows_ref, keep_ref, send_ref, early_ref):
    core = lax.axis_index("replica") % 2

    def rows(index):
        return rows_ref[pl.ds(index * BLOCK, BLOCK), :]

    halves = (((0, 0), (1, 0), (1, 1)), ((2, 0), (2, 1), (2, 2)))
    for mine in range(2):

        @pl.when(core == mine)
        def _():
            for place in range(3):
                kept, sent = halves[mine][place], halves[1 - mine][place]
                where = pl.ds(place * BLOCK, BLOCK)
                keep_ref[where, :] = dot_t(rows(kept[0]), rows(kept[1]))
                send_ref[where, :] = dot_t(rows(sent[0]), rows(sent[1])).astype(BF16)

    early_ref[...] = rows_ref[:, LATE:]


def partial_gram(rows):
    return pl.pallas_call(
        gram_kernel,
        out_shape=(
            jax.ShapeDtypeStruct((HALF, BLOCK), F32),
            jax.ShapeDtypeStruct((HALF, BLOCK), BF16),
            jax.ShapeDtypeStruct((FF, EARLY), BF16),
        ),
        in_specs=[VMEM],
        out_specs=(VMEM,) * 3,
        compiler_params=PARAMS,
    )(rows)


PIECE = HALF // 4


def chip_sum_kernel(keep_ref, got_ref, own_ref, next_ref, last_ref, far_ref):
    chip = lax.axis_index("replica") // 2

    def total(steps):
        where = pl.ds(pl.multiple_of(((chip + steps) % 4) * PIECE, PIECE), PIECE)
        return keep_ref[where, :] + got_ref[where, :].astype(F32)

    own_ref[...] = total(0)
    next_ref[...] = total(1).astype(BF16)
    last_ref[...] = total(3).astype(BF16)
    far_ref[...] = total(2).astype(BF16)


def chip_sum(keep, got):
    return pl.pallas_call(
        chip_sum_kernel,
        out_shape=(jax.ShapeDtypeStruct((PIECE, BLOCK), F32),)
        + (jax.ShapeDtypeStruct((PIECE, BLOCK), BF16),) * 3,
        in_specs=[VMEM, VMEM],
        out_specs=(VMEM,) * 4,
        compiler_params=PARAMS,
    )(keep, got)


def ring_sum_kernel(own_ref, a_ref, b_ref, c_ref, out_ref):
    total = own_ref[...] + a_ref[...].astype(F32) + b_ref[...].astype(F32) + c_ref[...].astype(F32)
    out_ref[...] = total.astype(BF16)


def ring_sum(own, first, second, third):
    return pl.pallas_call(
        ring_sum_kernel,
        out_shape=jax.ShapeDtypeStruct((PIECE, BLOCK), BF16),
        in_specs=[VMEM] * 4,
        out_specs=VMEM,
        compiler_params=PARAMS,
    )(own, first, second, third)


def chain_kernel(*refs):
    pieces, rows_ref, early_refs = refs[:8], refs[8], refs[9:13]
    late_out, early_out, packed, gram = refs[13:]
    index = lax.axis_index("replica")
    chip, core = index // 2, index % 2
    for steps in range(4):
        start = pl.multiple_of(((chip + steps) % 4) * PIECE, PIECE)
        packed[core, pl.ds(start, PIECE), :] = pieces[steps][...]
        packed[1 - core, pl.ds(start, PIECE), :] = pieces[4 + steps][...]
    row_id = lax.broadcasted_iota(jnp.int32, (BLOCK, BLOCK), 0)
    col_id = lax.broadcasted_iota(jnp.int32, (BLOCK, BLOCK), 1)
    diagonal = row_id == col_id
    places = ((0, 0), (1, 0), (1, 1), (2, 0), (2, 1), (2, 2))
    blocks = [packed[place // 3, pl.ds((place % 3) * BLOCK, BLOCK), :] for place in range(6)]
    squares = sum(
        jnp.sum(jnp.where(diagonal, block.astype(F32), 0.0))
        for block, (row, col) in zip(blocks, places)
        if row == col
    )
    squares = jnp.full((1, 1), squares, F32)
    scale = 1.0 / (jnp.sqrt(squares) + epsilon)
    for block, (row, col) in zip(blocks, places):
        scaled = (block.astype(F32) * scale) * scale
        gram[pl.ds(row * BLOCK, BLOCK), pl.ds(col * BLOCK, BLOCK)] = scaled.astype(BF16)
        if row != col:
            gram[pl.ds(col * BLOCK, BLOCK), pl.ds(row * BLOCK, BLOCK)] = scaled.T.astype(BF16)

    gram_0 = gram[...]
    poly_0 = (coef_gram * gram_0.astype(F32) + coef_square * dot(gram_0, gram_0)).astype(BF16)
    half_way = (coef_linear * gram_0.astype(F32) + dot(poly_0, gram_0)).astype(BF16)
    gram_1 = (coef_linear * half_way.astype(F32) + dot(half_way, poly_0)).astype(BF16)
    poly_1 = (coef_gram * gram_1.astype(F32) + coef_square * dot(gram_1, gram_1)).astype(BF16)

    def apply(rows):
        first = ((coef_linear * rows.astype(F32) + dot(poly_0, rows)) * scale).astype(BF16)
        second = coef_linear * first.astype(F32) + dot(poly_1, first)
        return (scale_factor * second).astype(BF16)

    late_out[...] = apply(rows_ref[:, :LATE])
    early_out[...] = apply(jnp.concatenate([ref[...] for ref in early_refs], axis=1))


def chain(pieces, rows, early):
    return pl.pallas_call(
        chain_kernel,
        out_shape=(
            jax.ShapeDtypeStruct((FF, LATE), BF16),
            jax.ShapeDtypeStruct((FF, 4 * EARLY), BF16),
        ),
        in_specs=[VMEM] * 13,
        out_specs=(VMEM, VMEM),
        scratch_shapes=[pltpu.VMEM((2, HALF, BLOCK), BF16), pltpu.VMEM((FF, FF), BF16)],
        compiler_params=PARAMS,
    )(*pieces, rows, *early)


def place_kernel(where, aliased, *refs):
    index = lax.axis_index("replica")
    chip, core = index // 2, index % 2
    count = len(where)
    pieces, out_ref, sems = refs[:count], refs[count + aliased], refs[count + aliased + 1]
    copies = []
    for number, (steps, cross, first, width, source) in enumerate(where):
        block = ((chip + steps) % 4) * 2 + (1 - core if cross else core)
        column = pl.multiple_of(block * WIDTH + first, 128)
        copies.append(
            pltpu.make_async_copy(
                pieces[number].at[:, :, pl.ds(source, width)],
                out_ref.at[:, :, pl.ds(column, width)],
                sems.at[number],
            )
        )
    for copy in copies:
        copy.start()
    for copy in copies:
        copy.wait()


def place(output, shape, pieces):
    arrays = [piece[0] for piece in pieces]
    where = tuple(piece[1:] for piece in pieces)
    aliased = output is not None
    anywhere = pl.BlockSpec(memory_space=pl.ANY)
    moved = sum(piece[4] for piece in pieces) * shape[0] * shape[1] * 4
    return pl.pallas_call(
        functools.partial(place_kernel, where, int(aliased)),
        out_shape=jax.ShapeDtypeStruct(shape, BF16),
        in_specs=[anywhere] * (len(arrays) + aliased),
        out_specs=anywhere,
        scratch_shapes=[pltpu.SemaphoreType.DMA((len(arrays),))],
        input_output_aliases={len(arrays): 0} if aliased else {},
        cost_estimate=pl.CostEstimate(flops=0, bytes_accessed=moved, transcendentals=0),
        compiler_params=PARAMS,
    )(*arrays, *([output] if aliased else []))


def local(gradient, momentum):
    new_momentum = momentum_decay * momentum + gradient.astype(F32)
    look_ahead = (gradient.astype(F32) + momentum_decay * new_momentum).astype(BF16)
    experts, pairs, row_count, col_count = look_ahead.shape
    flat_rows = look_ahead.reshape(experts * pairs, row_count, col_count)
    rows = lax.all_to_all(flat_rows, "tensor", split_axis=0, concat_axis=0, tiled=True)
    rows = rows.reshape(FF, col_count)

    keep, send, early = partial_gram(rows)
    own, to_next, to_last, to_far = chip_sum(keep, shift(send, 0, 1))
    mine = ring_sum(own, shift(to_next, 1), shift(to_last, -1), shift(to_far, 2))
    here = (mine, shift(mine, -1), shift(mine, 2), shift(mine, 1))
    other = tuple(shift(piece, 0, 1) for piece in here)
    early, _ = lax.optimization_barrier((early, mine))
    early = (early, shift(early, -1), shift(early, 2), shift(early, 1))
    late_rows, early_rows = chain(here + other, rows, early)

    def back(value):
        value = value.reshape(experts * pairs, row_count, value.shape[1])
        return lax.all_to_all(value, "tensor", split_axis=0, concat_axis=0, tiled=True)

    late = back(late_rows)
    late, early_rows = lax.optimization_barrier((late, early_rows))
    late_pieces = {0: late, 1: shift(late, -1), 3: shift(late, 1), 2: shift(late, 2)}
    late_across = {steps: shift(piece, 0, 1) for steps, piece in late_pieces.items()}
    early = back(early_rows)
    early_across = shift(early, 0, 1)

    shape = (experts * pairs, row_count, 8 * WIDTH)

    def late_place(pieces, steps, cross):
        return (pieces[steps], steps, cross, 0, LATE, 0)

    def early_places(value, cross):
        return [(value, steps, cross, LATE, EARLY, steps * EARLY) for steps in range(4)]

    update = place(
        None,
        shape,
        [late_place(late_pieces, 0, 0), late_place(late_across, 0, 1)] + early_places(early, 0),
    )
    update = place(
        update,
        shape,
        [late_place(late_pieces, steps, 0) for steps in (1, 2, 3)] + early_places(early_across, 1),
    )
    update = place(update, shape, [late_place(late_across, steps, 1) for steps in (1, 2, 3)])
    return (update.reshape(experts, pairs, row_count, 8 * WIDTH), new_momentum)


def solution(mesh):
    in_specs = (P(None, None, "tensor", "replica"), P(None, None, "tensor", "replica"))
    out_specs = (P(None, None, "tensor", None), P(None, None, "tensor", "replica"))
    return jax.shard_map(local, mesh=mesh, in_specs=in_specs, out_specs=out_specs, check_vma=False)
```

```python
import functools
import math

import jax
import jax.numpy as jnp
from jax import lax
from jax.experimental import pallas as pl
from jax.experimental.pallas import tpu as pltpu
from jax.sharding import PartitionSpec as P

D = 4096
FF = 768

momentum_decay = 0.95
coef_linear = 3.4445
coef_gram = -4.775
coef_square = 2.0315
epsilon = 1e-07
scale_factor = 0.2 * math.sqrt(max(FF, D))

WIDTH = 512
EARLY = 256
LATE = WIDTH - EARLY
BLOCK = 256
HALF = FF
VMEM = pl.BlockSpec(memory_space=pltpu.VMEM)
HBM = pl.BlockSpec(memory_space=pltpu.HBM)
PARAMS = pltpu.CompilerParams(vmem_limit_bytes=16 * 1024 * 1024)
LARGE = pltpu.CompilerParams(vmem_limit_bytes=32 * 1024 * 1024)
F32, BF16 = jnp.float32, jnp.bfloat16


def replica_place():
    index = lax.axis_index("replica")
    return index // 2, index % 2


def shift(value, steps, cross=0):
    pairs = [
        (chip * 2 + core, ((chip + steps) % 4) * 2 + (core ^ cross))
        for chip in range(4)
        for core in range(2)
    ]
    return lax.ppermute(value, "replica", pairs)


def dot_t(left, right):
    return lax.dot_general(left, right, (((1,), (1,)), ((), ())), preferred_element_type=F32)


def dot(left, right):
    return jnp.dot(left, right, preferred_element_type=F32)


def gram_kernel(rows_ref, keep_ref, send_ref, early_ref):
    core = lax.axis_index("replica") % 2

    def rows(index):
        return rows_ref[pl.ds(index * BLOCK, BLOCK), :]

    halves = (((0, 0), (1, 0), (1, 1)), ((2, 0), (2, 1), (2, 2)))
    for mine in range(2):

        @pl.when(core == mine)
        def _():
            for place in range(3):
                kept, sent = halves[mine][place], halves[1 - mine][place]
                where = pl.ds(place * BLOCK, BLOCK)
                keep_ref[where, :] = dot_t(rows(kept[0]), rows(kept[1]))
                send_ref[where, :] = dot_t(rows(sent[0]), rows(sent[1])).astype(BF16)

    early_ref[...] = rows_ref[:, LATE:]


def partial_gram(rows):
    return pl.pallas_call(
        gram_kernel,
        out_shape=(
            jax.ShapeDtypeStruct((HALF, BLOCK), F32),
            jax.ShapeDtypeStruct((HALF, BLOCK), BF16),
            jax.ShapeDtypeStruct((FF, EARLY), BF16),
        ),
        in_specs=[VMEM],
        out_specs=(VMEM,) * 3,
        compiler_params=PARAMS,
    )(rows)


PIECE = HALF // 4


def chip_sum_kernel(keep_ref, got_ref, own_ref, next_ref, last_ref, far_ref):
    chip = lax.axis_index("replica") // 2

    def total(steps):
        where = pl.ds(pl.multiple_of(((chip + steps) % 4) * PIECE, PIECE), PIECE)
        return keep_ref[where, :] + got_ref[where, :].astype(F32)

    own_ref[...] = total(0)
    next_ref[...] = total(1).astype(BF16)
    last_ref[...] = total(3).astype(BF16)
    far_ref[...] = total(2).astype(BF16)


def chip_sum(keep, got):
    return pl.pallas_call(
        chip_sum_kernel,
        out_shape=(jax.ShapeDtypeStruct((PIECE, BLOCK), F32),)
        + (jax.ShapeDtypeStruct((PIECE, BLOCK), BF16),) * 3,
        in_specs=[VMEM, VMEM],
        out_specs=(VMEM,) * 4,
        compiler_params=PARAMS,
    )(keep, got)


def ring_sum_kernel(own_ref, a_ref, b_ref, c_ref, out_ref):
    total = own_ref[...] + a_ref[...].astype(F32) + b_ref[...].astype(F32) + c_ref[...].astype(F32)
    out_ref[...] = total.astype(BF16)


def ring_sum(own, first, second, third):
    return pl.pallas_call(
        ring_sum_kernel,
        out_shape=jax.ShapeDtypeStruct((PIECE, BLOCK), BF16),
        in_specs=[VMEM] * 4,
        out_specs=VMEM,
        compiler_params=PARAMS,
    )(own, first, second, third)


def chain_kernel(*refs):
    pieces, rows_ref = refs[:8], refs[8]
    out_ref, polys_out, scale_ref, packed, gram, polys, sems = refs[9:]
    index = lax.axis_index("replica")
    chip, core = index // 2, index % 2
    for steps in range(4):
        start = pl.multiple_of(((chip + steps) % 4) * PIECE, PIECE)
        packed[core, pl.ds(start, PIECE), :] = pieces[steps][...]
        packed[1 - core, pl.ds(start, PIECE), :] = pieces[4 + steps][...]
    row_id = lax.broadcasted_iota(jnp.int32, (BLOCK, BLOCK), 0)
    col_id = lax.broadcasted_iota(jnp.int32, (BLOCK, BLOCK), 1)
    diagonal = row_id == col_id
    places = ((0, 0), (1, 0), (1, 1), (2, 0), (2, 1), (2, 2))
    blocks = [packed[place // 3, pl.ds((place % 3) * BLOCK, BLOCK), :] for place in range(6)]
    squares = sum(
        jnp.sum(jnp.where(diagonal, block.astype(F32), 0.0))
        for block, (row, col) in zip(blocks, places)
        if row == col
    )
    squares = jnp.full((1, 1), squares, F32)
    scale = 1.0 / (jnp.sqrt(squares) + epsilon)
    for block, (row, col) in zip(blocks, places):
        scaled = (block.astype(F32) * scale) * scale
        gram[pl.ds(row * BLOCK, BLOCK), pl.ds(col * BLOCK, BLOCK)] = scaled.astype(BF16)
        if row != col:
            gram[pl.ds(col * BLOCK, BLOCK), pl.ds(row * BLOCK, BLOCK)] = scaled.T.astype(BF16)

    gram_0 = gram[...]
    poly_0 = (coef_gram * gram_0.astype(F32) + coef_square * dot(gram_0, gram_0)).astype(BF16)
    half_way = (coef_linear * gram_0.astype(F32) + dot(poly_0, gram_0)).astype(BF16)
    gram_1 = (coef_linear * half_way.astype(F32) + dot(half_way, poly_0)).astype(BF16)
    poly_1 = (coef_gram * gram_1.astype(F32) + coef_square * dot(gram_1, gram_1)).astype(BF16)
    polys[0] = poly_0
    polys[1] = poly_1
    scale_ref[...] = jnp.broadcast_to(scale, scale_ref.shape)
    keep = pltpu.make_async_copy(polys, polys_out, sems.at[0])
    keep.start()
    out_ref[...] = both_steps(poly_0, poly_1, scale, rows_ref[:, :LATE])
    keep.wait()


def both_steps(poly_0, poly_1, scale, rows):
    first = ((coef_linear * rows.astype(F32) + dot(poly_0, rows)) * scale).astype(BF16)
    second = coef_linear * first.astype(F32) + dot(poly_1, first)
    return (scale_factor * second).astype(BF16)


def chain(pieces, rows):
    return pl.pallas_call(
        chain_kernel,
        out_shape=(
            jax.ShapeDtypeStruct((FF, LATE), BF16),
            jax.ShapeDtypeStruct((2, FF, FF), BF16),
            jax.ShapeDtypeStruct((8, 128), F32),
        ),
        in_specs=[VMEM] * 9,
        out_specs=(VMEM, HBM, VMEM),
        scratch_shapes=[
            pltpu.VMEM((2, HALF, BLOCK), BF16),
            pltpu.VMEM((FF, FF), BF16),
            pltpu.VMEM((2, FF, FF), BF16),
            pltpu.SemaphoreType.DMA((1,)),
        ],
        compiler_params=LARGE,
    )(*pieces, rows)


def early_kernel(polys_in, scale_ref, *refs):
    early_in, out_ref, polys, early, sems = refs[:4], refs[4], refs[5], refs[6], refs[7]
    copies = [pltpu.make_async_copy(polys_in, polys, sems.at[4])]
    for steps in range(4):
        copies.append(pltpu.make_async_copy(early_in[steps], early.at[steps], sems.at[steps]))
    for copy in copies:
        copy.start()
    copies[0].wait()
    for steps in range(4):
        copies[1 + steps].wait()
        out_ref[:, pl.ds(steps * EARLY, EARLY)] = both_steps(
            polys[0], polys[1], scale_ref[:1, :1], early[steps]
        )


def early_products(polys, scale, early):
    flops = 2 * 2 * FF * FF * 4 * EARLY
    return pl.pallas_call(
        early_kernel,
        out_shape=jax.ShapeDtypeStruct((FF, 4 * EARLY), BF16),
        in_specs=[HBM, VMEM] + [HBM] * 4,
        out_specs=VMEM,
        scratch_shapes=[
            pltpu.VMEM((2, FF, FF), BF16),
            pltpu.VMEM((4, FF, EARLY), BF16),
            pltpu.SemaphoreType.DMA((5,)),
        ],
        cost_estimate=pl.CostEstimate(flops=flops, bytes_accessed=0, transcendentals=0),
        compiler_params=LARGE,
    )(polys, scale, *early)


def place_kernel(where, aliased, *refs):
    index = lax.axis_index("replica")
    chip, core = index // 2, index % 2
    count = len(where)
    pieces, out_ref, sems = refs[:count], refs[count + aliased], refs[count + aliased + 1]
    copies = []
    for number, (steps, cross, first, width, source) in enumerate(where):
        block = ((chip + steps) % 4) * 2 + (1 - core if cross else core)
        column = pl.multiple_of(block * WIDTH + first, 128)
        copies.append(
            pltpu.make_async_copy(
                pieces[number].at[:, :, pl.ds(source, width)],
                out_ref.at[:, :, pl.ds(column, width)],
                sems.at[number],
            )
        )
    for copy in copies:
        copy.start()
    for copy in copies:
        copy.wait()


def place(output, shape, pieces):
    arrays = [piece[0] for piece in pieces]
    where = tuple(piece[1:] for piece in pieces)
    aliased = output is not None
    anywhere = pl.BlockSpec(memory_space=pl.ANY)
    return pl.pallas_call(
        functools.partial(place_kernel, where, int(aliased)),
        out_shape=jax.ShapeDtypeStruct(shape, BF16),
        in_specs=[anywhere] * (len(arrays) + aliased),
        out_specs=anywhere,
        scratch_shapes=[pltpu.SemaphoreType.DMA((len(arrays),))],
        input_output_aliases={len(arrays): 0} if aliased else {},
        cost_estimate=pl.CostEstimate(flops=0, bytes_accessed=0, transcendentals=0),
        compiler_params=PARAMS,
    )(*arrays, *([output] if aliased else []))


def local(gradient, momentum):
    def stepped(gradient, momentum):
        return momentum_decay * momentum + gradient.astype(F32)

    ahead = gradient.astype(F32) + momentum_decay * stepped(gradient, momentum)
    experts, pairs, row_count, col_count = gradient.shape
    flat_rows = ahead.astype(BF16).reshape(experts * pairs, row_count, col_count)
    rows = lax.all_to_all(flat_rows, "tensor", split_axis=0, concat_axis=0, tiled=True)
    rows = rows.reshape(FF, col_count)

    keep, send, early = partial_gram(rows)
    own, to_next, to_last, to_far = chip_sum(keep, shift(send, 0, 1))
    mine = ring_sum(own, shift(to_next, 1), shift(to_last, -1), shift(to_far, 2))
    here = (mine, shift(mine, -1), shift(mine, 2), shift(mine, 1))
    other = tuple(shift(piece, 0, 1) for piece in here)
    late_rows, polys, scale = chain(here + other, rows)

    def back(value):
        value = value.reshape(experts * pairs, row_count, value.shape[1])
        return lax.all_to_all(value, "tensor", split_axis=0, concat_axis=0, tiled=True)

    gradient, momentum, late_rows = lax.optimization_barrier((gradient, momentum, late_rows))
    new_momentum = stepped(gradient, momentum)
    early, _ = lax.optimization_barrier((early, here[2]))
    early = (early, shift(early, -1), shift(early, 2), shift(early, 1))
    early_rows = early_products(polys, scale, early)
    late = back(late_rows)
    late, early_rows, new_momentum = lax.optimization_barrier((late, early_rows, new_momentum))
    late_pieces = {0: late, 1: shift(late, -1), 3: shift(late, 1), 2: shift(late, 2)}
    early = back(early_rows)

    shape = (experts * pairs, row_count, 8 * WIDTH)

    def late_place(pieces, steps, cross):
        return (pieces[steps], steps, cross, 0, LATE, 0)

    def early_place(value, cross):
        return [(value, steps, cross, LATE, EARLY, steps * EARLY) for steps in range(4)]

    late_across = {steps: shift(piece, 0, 1) for steps, piece in late_pieces.items()}
    update = place(None, shape, [late_place(late_pieces, 0, 0), late_place(late_across, 0, 1)])
    update = place(update, shape, [late_place(late_pieces, steps, 0) for steps in (1, 2, 3)])
    update = place(update, shape, [late_place(late_across, steps, 1) for steps in (1, 2, 3)])
    early, update = lax.optimization_barrier((early, update))
    update = place(update, shape, early_place(early, 0))
    update = place(update, shape, early_place(shift(early, 0, 1), 1))
    return (update.reshape(experts, pairs, row_count, 8 * WIDTH), new_momentum)


def solution(mesh):
    in_specs = (P(None, None, "tensor", "replica"), P(None, None, "tensor", "replica"))
    out_specs = (P(None, None, "tensor", None), P(None, None, "tensor", "replica"))
    return jax.shard_map(local, mesh=mesh, in_specs=in_specs, out_specs=out_specs, check_vma=False)
```

```python
import functools
import math

import jax
import jax.numpy as jnp
from jax import lax
from jax.experimental import pallas as pl
from jax.experimental.pallas import tpu as pltpu
from jax.sharding import PartitionSpec as P

D = 4096
FF = 768

momentum_decay = 0.95
coef_linear = 3.4445
coef_gram = -4.775
coef_square = 2.0315
epsilon = 1e-07
scale_factor = 0.2 * math.sqrt(max(FF, D))

WIDTH = 512
EARLY = 256
LATE = WIDTH - EARLY
BLOCK = 256
HALF = FF
VMEM = pl.BlockSpec(memory_space=pltpu.VMEM)
HBM = pl.BlockSpec(memory_space=pltpu.HBM)
PARAMS = pltpu.CompilerParams(vmem_limit_bytes=16 * 1024 * 1024)
LARGE = pltpu.CompilerParams(vmem_limit_bytes=32 * 1024 * 1024)
F32, BF16 = jnp.float32, jnp.bfloat16


def replica_place():
    index = lax.axis_index("replica")
    return index // 2, index % 2


def shift(value, steps, cross=0):
    pairs = [
        (chip * 2 + core, ((chip + steps) % 4) * 2 + (core ^ cross))
        for chip in range(4)
        for core in range(2)
    ]
    return lax.ppermute(value, "replica", pairs)


def dot_t(left, right):
    return lax.dot_general(left, right, (((1,), (1,)), ((), ())), preferred_element_type=F32)


def dot(left, right):
    return jnp.dot(left, right, preferred_element_type=F32)


def gram_kernel(rows_ref, keep_ref, send_ref, early_ref):
    core = lax.axis_index("replica") % 2

    def rows(index):
        return rows_ref[pl.ds(index * BLOCK, BLOCK), :]

    halves = (((0, 0), (1, 0), (1, 1)), ((2, 0), (2, 1), (2, 2)))
    for mine in range(2):

        @pl.when(core == mine)
        def _():
            for place in range(3):
                kept, sent = halves[mine][place], halves[1 - mine][place]
                where = pl.ds(place * BLOCK, BLOCK)
                keep_ref[where, :] = dot_t(rows(kept[0]), rows(kept[1]))
                send_ref[where, :] = dot_t(rows(sent[0]), rows(sent[1])).astype(BF16)

    early_ref[...] = rows_ref[:, LATE:]


def partial_gram(rows):
    return pl.pallas_call(
        gram_kernel,
        out_shape=(
            jax.ShapeDtypeStruct((HALF, BLOCK), F32),
            jax.ShapeDtypeStruct((HALF, BLOCK), BF16),
            jax.ShapeDtypeStruct((FF, EARLY), BF16),
        ),
        in_specs=[VMEM],
        out_specs=(VMEM,) * 3,
        compiler_params=PARAMS,
    )(rows)


PIECE = HALF // 4


def chip_sum_kernel(keep_ref, got_ref, own_ref, next_ref, last_ref, far_ref):
    chip = lax.axis_index("replica") // 2

    def total(steps):
        where = pl.ds(pl.multiple_of(((chip + steps) % 4) * PIECE, PIECE), PIECE)
        return keep_ref[where, :] + got_ref[where, :].astype(F32)

    own_ref[...] = total(0)
    next_ref[...] = total(1).astype(BF16)
    last_ref[...] = total(3).astype(BF16)
    far_ref[...] = total(2).astype(BF16)


def chip_sum(keep, got):
    return pl.pallas_call(
        chip_sum_kernel,
        out_shape=(jax.ShapeDtypeStruct((PIECE, BLOCK), F32),)
        + (jax.ShapeDtypeStruct((PIECE, BLOCK), BF16),) * 3,
        in_specs=[VMEM, VMEM],
        out_specs=(VMEM,) * 4,
        compiler_params=PARAMS,
    )(keep, got)


def ring_sum_kernel(own_ref, a_ref, b_ref, c_ref, out_ref):
    total = own_ref[...] + a_ref[...].astype(F32) + b_ref[...].astype(F32) + c_ref[...].astype(F32)
    out_ref[...] = total.astype(BF16)


def ring_sum(own, first, second, third):
    return pl.pallas_call(
        ring_sum_kernel,
        out_shape=jax.ShapeDtypeStruct((PIECE, BLOCK), BF16),
        in_specs=[VMEM] * 4,
        out_specs=VMEM,
        compiler_params=PARAMS,
    )(own, first, second, third)


def chain_kernel(*refs):
    pieces, rows_ref = refs[:8], refs[8]
    out_ref, polys_out, scale_ref, packed, gram, polys, late, sems = refs[9:]
    index = lax.axis_index("replica")
    chip, core = index // 2, index % 2
    for steps in range(4):
        start = pl.multiple_of(((chip + steps) % 4) * PIECE, PIECE)
        packed[core, pl.ds(start, PIECE), :] = pieces[steps][...]
        packed[1 - core, pl.ds(start, PIECE), :] = pieces[4 + steps][...]
    row_id = lax.broadcasted_iota(jnp.int32, (BLOCK, BLOCK), 0)
    col_id = lax.broadcasted_iota(jnp.int32, (BLOCK, BLOCK), 1)
    diagonal = row_id == col_id
    places = ((0, 0), (1, 0), (1, 1), (2, 0), (2, 1), (2, 2))
    blocks = [packed[place // 3, pl.ds((place % 3) * BLOCK, BLOCK), :] for place in range(6)]
    squares = sum(
        jnp.sum(jnp.where(diagonal, block.astype(F32), 0.0))
        for block, (row, col) in zip(blocks, places)
        if row == col
    )
    squares = jnp.full((1, 1), squares, F32)
    scale = 1.0 / (jnp.sqrt(squares) + epsilon)
    for block, (row, col) in zip(blocks, places):
        scaled = (block.astype(F32) * scale) * scale
        gram[pl.ds(row * BLOCK, BLOCK), pl.ds(col * BLOCK, BLOCK)] = scaled.astype(BF16)
        if row != col:
            gram[pl.ds(col * BLOCK, BLOCK), pl.ds(row * BLOCK, BLOCK)] = scaled.T.astype(BF16)

    def keep(value, place):
        polys[place] = value
        copy = pltpu.make_async_copy(polys.at[place], polys_out.at[place], sems.at[place])
        copy.start()
        return copy

    scale_ref[...] = jnp.broadcast_to(scale, scale_ref.shape)
    gram_0 = gram[...]
    poly_0 = (coef_gram * gram_0.astype(F32) + coef_square * dot(gram_0, gram_0)).astype(BF16)
    copies = [keep(poly_0, 0)]
    half_way = (coef_linear * gram_0.astype(F32) + dot(poly_0, gram_0)).astype(BF16)
    gram_1 = (coef_linear * half_way.astype(F32) + dot(half_way, poly_0)).astype(BF16)
    poly_1 = (coef_gram * gram_1.astype(F32) + coef_square * dot(gram_1, gram_1)).astype(BF16)
    copies.append(keep(poly_1, 1))
    rows = rows_ref[:, :LATE]
    first = ((coef_linear * rows.astype(F32) + dot(poly_0, rows)) * scale).astype(BF16)
    for block in range(FF // BLOCK):
        where = pl.ds(block * BLOCK, BLOCK)
        cut = slice(block * BLOCK, (block + 1) * BLOCK)
        second = coef_linear * first[cut].astype(F32) + dot(poly_1[cut], first)
        late[where, :] = (scale_factor * second).astype(BF16)
        copies.append(
            pltpu.make_async_copy(late.at[where, :], out_ref.at[where, :], sems.at[2 + block])
        )
        copies[-1].start()
    for copy in copies:
        copy.wait()


def chain(pieces, rows):
    return pl.pallas_call(
        chain_kernel,
        out_shape=(
            jax.ShapeDtypeStruct((FF, LATE), BF16),
            pltpu.HBM((2, FF, FF), BF16),
            jax.ShapeDtypeStruct((8, 128), F32),
        ),
        in_specs=[VMEM] * 9,
        out_specs=(HBM, HBM, VMEM),
        scratch_shapes=[
            pltpu.VMEM((2, HALF, BLOCK), BF16),
            pltpu.VMEM((FF, FF), BF16),
            pltpu.VMEM((2, FF, FF), BF16),
            pltpu.VMEM((FF, LATE), BF16),
            pltpu.SemaphoreType.DMA((5,)),
        ],
        cost_estimate=pl.CostEstimate(flops=0, bytes_accessed=0, transcendentals=0),
        compiler_params=LARGE,
    )(*pieces, rows)


def both_steps_at_once(square, scale, rows):
    total = coef_linear * coef_linear * rows.astype(F32) + dot(square, rows)
    return ((scale_factor * scale) * total).astype(BF16)


def own_kernel(polys_in, scale_ref, early_in, out_ref, square_out, polys, early, square, result, sems):
    loads = [pltpu.make_async_copy(polys_in.at[i], polys.at[i], sems.at[i]) for i in range(2)]
    loads.append(pltpu.make_async_copy(early_in, early, sems.at[2]))
    for load in loads:
        load.start()
    for load in loads:
        load.wait()
    sums = polys[0].astype(F32) + polys[1].astype(F32)
    square[...] = (coef_linear * sums + dot(polys[1], polys[0])).astype(BF16)
    stores = [pltpu.make_async_copy(square, square_out, sems.at[3])]
    stores[0].start()
    result[...] = both_steps_at_once(square[...], scale_ref[:1, :1], early[...])
    stores.append(pltpu.make_async_copy(result, out_ref.at[:, pl.ds(0, EARLY)], sems.at[4]))
    stores[1].start()
    for store in stores:
        store.wait()


def other_kernel(square_ref, scale_ref, *refs):
    early_in, out_ref, result, sems = refs[:3], *refs[4:]
    stores = []
    for place in range(3):
        result[place] = both_steps_at_once(
            square_ref[...], scale_ref[:1, :1], early_in[place][...]
        )
        where = out_ref.at[:, pl.ds((1 + place) * EARLY, EARLY)]
        stores.append(pltpu.make_async_copy(result.at[place], where, sems.at[place]))
        stores[-1].start()
    for store in stores:
        store.wait()


def early_products(polys, scale, early):
    out = jax.ShapeDtypeStruct((FF, 4 * EARLY), BF16)
    flops = 2 * FF * FF * EARLY
    result, square = pl.pallas_call(
        own_kernel,
        out_shape=(out, pltpu.HBM((FF, FF), BF16)),
        in_specs=[HBM, VMEM, HBM],
        out_specs=(HBM, HBM),
        scratch_shapes=[
            pltpu.VMEM((2, FF, FF), BF16),
            pltpu.VMEM((FF, EARLY), BF16),
            pltpu.VMEM((FF, FF), BF16),
            pltpu.VMEM((FF, EARLY), BF16),
            pltpu.SemaphoreType.DMA((5,)),
        ],
        cost_estimate=pl.CostEstimate(flops=4 * flops, bytes_accessed=0, transcendentals=0),
        compiler_params=LARGE,
    )(polys, scale, early[0])
    return pl.pallas_call(
        other_kernel,
        out_shape=out,
        in_specs=[VMEM] * 5 + [HBM],
        out_specs=HBM,
        scratch_shapes=[pltpu.VMEM((3, FF, EARLY), BF16), pltpu.SemaphoreType.DMA((3,))],
        input_output_aliases={5: 0},
        cost_estimate=pl.CostEstimate(flops=3 * flops, bytes_accessed=0, transcendentals=0),
        compiler_params=LARGE,
    )(square, scale, *early[1:], result)


def place_kernel(where, aliased, *refs):
    index = lax.axis_index("replica")
    chip, core = index // 2, index % 2
    count = len(where)
    pieces, out_ref, sems = refs[:count], refs[count + aliased], refs[count + aliased + 1]
    copies = []
    for number, (steps, cross, first, width, source) in enumerate(where):
        block = ((chip + steps) % 4) * 2 + (1 - core if cross else core)
        column = pl.multiple_of(block * WIDTH + first, 128)
        copies.append(
            pltpu.make_async_copy(
                pieces[number].at[:, :, pl.ds(source, width)],
                out_ref.at[:, :, pl.ds(column, width)],
                sems.at[number],
            )
        )
    for copy in copies:
        copy.start()
    for copy in copies:
        copy.wait()


def place(output, shape, pieces):
    arrays = [piece[0] for piece in pieces]
    where = tuple(piece[1:] for piece in pieces)
    aliased = output is not None
    anywhere = pl.BlockSpec(memory_space=pl.ANY)
    return pl.pallas_call(
        functools.partial(place_kernel, where, int(aliased)),
        out_shape=jax.ShapeDtypeStruct(shape, BF16),
        in_specs=[anywhere] * (len(arrays) + aliased),
        out_specs=anywhere,
        scratch_shapes=[pltpu.SemaphoreType.DMA((len(arrays),))],
        input_output_aliases={len(arrays): 0} if aliased else {},
        cost_estimate=pl.CostEstimate(flops=0, bytes_accessed=0, transcendentals=0),
        compiler_params=PARAMS,
    )(*arrays, *([output] if aliased else []))


def local(gradient, momentum):
    def stepped(gradient, momentum):
        return momentum_decay * momentum + gradient.astype(F32)

    ahead = gradient.astype(F32) + momentum_decay * stepped(gradient, momentum)
    experts, pairs, row_count, col_count = gradient.shape
    flat_rows = ahead.astype(BF16).reshape(experts * pairs, row_count, col_count)
    rows = lax.all_to_all(flat_rows, "tensor", split_axis=0, concat_axis=0, tiled=True)
    rows = rows.reshape(FF, col_count)

    keep, send, early = partial_gram(rows)
    own, to_next, to_last, to_far = chip_sum(keep, shift(send, 0, 1))
    mine = ring_sum(own, shift(to_next, 1), shift(to_last, -1), shift(to_far, 2))
    here = (mine, shift(mine, -1), shift(mine, 2), shift(mine, 1))
    other = tuple(shift(piece, 0, 1) for piece in here)
    late_rows, polys, scale = chain(here + other, rows)

    def back(value):
        value = value.reshape(experts * pairs, row_count, value.shape[1])
        return lax.all_to_all(value, "tensor", split_axis=0, concat_axis=0, tiled=True)

    gradient, momentum, late_rows = lax.optimization_barrier((gradient, momentum, late_rows))
    new_momentum = stepped(gradient, momentum)
    early, _ = lax.optimization_barrier((early, here[2]))
    early = (early, shift(early, -1), shift(early, 2), shift(early, 1))
    early_rows = early_products(polys, scale, early)
    late = back(late_rows)
    late, early_rows, new_momentum = lax.optimization_barrier((late, early_rows, new_momentum))
    late_pieces = {0: late, 1: shift(late, -1), 3: shift(late, 1), 2: shift(late, 2)}
    early = back(early_rows)

    shape = (experts * pairs, row_count, 8 * WIDTH)

    def late_place(pieces, steps, cross):
        return (pieces[steps], steps, cross, 0, LATE, 0)

    def early_place(value, steps, cross, source):
        return (value, steps, cross, LATE, EARLY, source)

    late_across = {0: shift(late, 0, 1)}
    update = place(None, shape, [late_place(late_pieces, 0, 0), late_place(late_across, 0, 1)])
    for steps in (1, 3, 2):
        late_pieces[steps], update = lax.optimization_barrier((late_pieces[steps], update))
        late_across[steps] = shift(late_pieces[steps], 0, 1)
    update = place(update, shape, [late_place(late_pieces, steps, 0) for steps in (1, 3, 2)])
    update = place(update, shape, [late_place(late_across, steps, 1) for steps in (1, 3, 2)])
    early, update = lax.optimization_barrier((early, update))
    across = [shift(early[:, :, cut : cut + 2 * EARLY], 0, 1) for cut in (0, 2 * EARLY)]
    update = place(update, shape, [early_place(early, steps, 0, steps * EARLY) for steps in range(4)])
    for half in range(2):
        places = [early_place(across[half], 2 * half + i, 1, i * EARLY) for i in range(2)]
        update = place(update, shape, places)
    return (update.reshape(experts, pairs, row_count, 8 * WIDTH), new_momentum)


def solution(mesh):
    in_specs = (P(None, None, "tensor", "replica"), P(None, None, "tensor", "replica"))
    out_specs = (P(None, None, "tensor", None), P(None, None, "tensor", "replica"))
    return jax.shard_map(local, mesh=mesh, in_specs=in_specs, out_specs=out_specs, check_vma=False)
```

```python
import functools
import math

import jax
import jax.numpy as jnp
from jax import lax
from jax.experimental import pallas as pl
from jax.experimental.pallas import tpu as pltpu
from jax.sharding import PartitionSpec as P

D = 4096
FF = 768

momentum_decay = 0.95
coef_linear = 3.4445
coef_gram = -4.775
coef_square = 2.0315
epsilon = 1e-07
scale_factor = 0.2 * math.sqrt(max(FF, D))

WIDTH = 512
LATE, MIDDLE, EARLY = 256, 0, 256
FIRST = LATE + MIDDLE
NEAR = MIDDLE + EARLY
SECOND = 2 * NEAR + 2 * EARLY
BLOCK = 256
HALF = FF
VMEM = pl.BlockSpec(memory_space=pltpu.VMEM)
HBM = pl.BlockSpec(memory_space=pltpu.HBM)
PARAMS = pltpu.CompilerParams(vmem_limit_bytes=16 * 1024 * 1024)
LARGE = pltpu.CompilerParams(vmem_limit_bytes=32 * 1024 * 1024)
F32, BF16 = jnp.float32, jnp.bfloat16


def replica_place():
    index = lax.axis_index("replica")
    return index // 2, index % 2


def shift(value, steps, cross=0):
    pairs = [
        (chip * 2 + core, ((chip + steps) % 4) * 2 + (core ^ cross))
        for chip in range(4)
        for core in range(2)
    ]
    return lax.ppermute(value, "replica", pairs)


def dot_t(left, right):
    return lax.dot_general(left, right, (((1,), (1,)), ((), ())), preferred_element_type=F32)


def dot(left, right):
    return jnp.dot(left, right, preferred_element_type=F32)


def gram_kernel(rows_ref, keep_ref, send_ref, near_ref, far_ref):
    core = lax.axis_index("replica") % 2

    def rows(index):
        return rows_ref[pl.ds(index * BLOCK, BLOCK), :]

    halves = (((0, 0), (1, 0), (1, 1)), ((2, 0), (2, 1), (2, 2)))
    for mine in range(2):

        @pl.when(core == mine)
        def _():
            for place in range(3):
                kept, sent = halves[mine][place], halves[1 - mine][place]
                where = pl.ds(place * BLOCK, BLOCK)
                keep_ref[where, :] = dot_t(rows(kept[0]), rows(kept[1]))
                send_ref[where, :] = dot_t(rows(sent[0]), rows(sent[1])).astype(BF16)

    near_ref[...] = rows_ref[:, LATE:]
    far_ref[...] = rows_ref[:, FIRST:]


def partial_gram(rows):
    return pl.pallas_call(
        gram_kernel,
        out_shape=(
            jax.ShapeDtypeStruct((HALF, BLOCK), F32),
            jax.ShapeDtypeStruct((HALF, BLOCK), BF16),
            jax.ShapeDtypeStruct((FF, NEAR), BF16),
            jax.ShapeDtypeStruct((FF, EARLY), BF16),
        ),
        in_specs=[VMEM],
        out_specs=(VMEM,) * 4,
        compiler_params=PARAMS,
    )(rows)


PIECE = HALF // 4


def chip_sum_kernel(keep_ref, got_ref, own_ref, next_ref, last_ref, far_ref):
    chip = lax.axis_index("replica") // 2

    def total(steps):
        where = pl.ds(pl.multiple_of(((chip + steps) % 4) * PIECE, PIECE), PIECE)
        return keep_ref[where, :] + got_ref[where, :].astype(F32)

    own_ref[...] = total(0)
    next_ref[...] = total(1).astype(BF16)
    last_ref[...] = total(3).astype(BF16)
    far_ref[...] = total(2).astype(BF16)


def chip_sum(keep, got):
    return pl.pallas_call(
        chip_sum_kernel,
        out_shape=(jax.ShapeDtypeStruct((PIECE, BLOCK), F32),)
        + (jax.ShapeDtypeStruct((PIECE, BLOCK), BF16),) * 3,
        in_specs=[VMEM, VMEM],
        out_specs=(VMEM,) * 4,
        compiler_params=PARAMS,
    )(keep, got)


def ring_sum_kernel(own_ref, a_ref, b_ref, c_ref, out_ref):
    total = own_ref[...] + a_ref[...].astype(F32) + b_ref[...].astype(F32) + c_ref[...].astype(F32)
    out_ref[...] = total.astype(BF16)


def ring_sum(own, first, second, third):
    return pl.pallas_call(
        ring_sum_kernel,
        out_shape=jax.ShapeDtypeStruct((PIECE, BLOCK), BF16),
        in_specs=[VMEM] * 4,
        out_specs=VMEM,
        compiler_params=PARAMS,
    )(own, first, second, third)


def chain_kernel(*refs):
    pieces, rows_ref = refs[:8], refs[8]
    out_ref, polys_out, scale_ref, packed, gram, polys, late, sems = refs[9:]
    index = lax.axis_index("replica")
    chip, core = index // 2, index % 2
    for steps in range(4):
        start = pl.multiple_of(((chip + steps) % 4) * PIECE, PIECE)
        packed[core, pl.ds(start, PIECE), :] = pieces[steps][...]
        packed[1 - core, pl.ds(start, PIECE), :] = pieces[4 + steps][...]
    row_id = lax.broadcasted_iota(jnp.int32, (BLOCK, BLOCK), 0)
    col_id = lax.broadcasted_iota(jnp.int32, (BLOCK, BLOCK), 1)
    diagonal = row_id == col_id
    places = ((0, 0), (1, 0), (1, 1), (2, 0), (2, 1), (2, 2))
    blocks = [packed[place // 3, pl.ds((place % 3) * BLOCK, BLOCK), :] for place in range(6)]
    squares = sum(
        jnp.sum(jnp.where(diagonal, block.astype(F32), 0.0))
        for block, (row, col) in zip(blocks, places)
        if row == col
    )
    squares = jnp.full((1, 1), squares, F32)
    scale = 1.0 / (jnp.sqrt(squares) + epsilon)
    for block, (row, col) in zip(blocks, places):
        scaled = (block.astype(F32) * scale) * scale
        gram[pl.ds(row * BLOCK, BLOCK), pl.ds(col * BLOCK, BLOCK)] = scaled.astype(BF16)
        if row != col:
            gram[pl.ds(col * BLOCK, BLOCK), pl.ds(row * BLOCK, BLOCK)] = scaled.T.astype(BF16)

    def keep(value, place):
        polys[place] = value
        copy = pltpu.make_async_copy(polys.at[place], polys_out.at[place], sems.at[place])
        copy.start()
        return copy

    scale_ref[...] = jnp.broadcast_to(scale, scale_ref.shape)
    gram_0 = gram[...]
    poly_0 = (coef_gram * gram_0.astype(F32) + coef_square * dot(gram_0, gram_0)).astype(BF16)
    copies = [keep(poly_0, 0)]
    half_way = (coef_linear * gram_0.astype(F32) + dot(poly_0, gram_0)).astype(BF16)
    gram_1 = (coef_linear * half_way.astype(F32) + dot(half_way, poly_0)).astype(BF16)
    poly_1 = (coef_gram * gram_1.astype(F32) + coef_square * dot(gram_1, gram_1)).astype(BF16)
    copies.append(keep(poly_1, 1))
    rows = rows_ref[:, :FIRST]
    first = ((coef_linear * rows.astype(F32) + dot(poly_0, rows)) * scale).astype(BF16)
    for block in range(FF // BLOCK):
        where = pl.ds(block * BLOCK, BLOCK)
        cut = slice(block * BLOCK, (block + 1) * BLOCK)
        second = coef_linear * first[cut].astype(F32) + dot(poly_1[cut], first)
        late[where, :] = (scale_factor * second).astype(BF16)
        copies.append(
            pltpu.make_async_copy(late.at[where, :], out_ref.at[where, :], sems.at[2 + block])
        )
        copies[-1].start()
    for copy in copies:
        copy.wait()


def chain(pieces, rows):
    return pl.pallas_call(
        chain_kernel,
        out_shape=(
            jax.ShapeDtypeStruct((FF, FIRST), BF16),
            pltpu.HBM((2, FF, FF), BF16),
            jax.ShapeDtypeStruct((8, 128), F32),
        ),
        in_specs=[VMEM] * 9,
        out_specs=(HBM, HBM, VMEM),
        scratch_shapes=[
            pltpu.VMEM((2, HALF, BLOCK), BF16),
            pltpu.VMEM((FF, FF), BF16),
            pltpu.VMEM((2, FF, FF), BF16),
            pltpu.VMEM((FF, FIRST), BF16),
            pltpu.SemaphoreType.DMA((5,)),
        ],
        cost_estimate=pl.CostEstimate(flops=0, bytes_accessed=0, transcendentals=0),
        compiler_params=LARGE,
    )(*pieces, rows)


def both_steps_at_once(square, scale, rows):
    total = coef_linear * coef_linear * rows.astype(F32) + dot(square, rows)
    return ((scale_factor * scale) * total).astype(BF16)


def own_kernel(polys_in, scale_ref, early_in, out_ref, square_out, polys, early, square, result, sems):
    loads = [pltpu.make_async_copy(polys_in.at[i], polys.at[i], sems.at[i]) for i in range(2)]
    loads.append(pltpu.make_async_copy(early_in, early, sems.at[2]))
    for load in loads:
        load.start()
    for load in loads:
        load.wait()
    sums = polys[0].astype(F32) + polys[1].astype(F32)
    square[...] = (coef_linear * sums + dot(polys[1], polys[0])).astype(BF16)
    stores = [pltpu.make_async_copy(square, square_out, sems.at[3])]
    stores[0].start()
    result[...] = both_steps_at_once(square[...], scale_ref[:1, :1], early[...])
    stores.append(pltpu.make_async_copy(result, out_ref.at[:, pl.ds(0, EARLY)], sems.at[4]))
    stores[1].start()
    for store in stores:
        store.wait()


ORDER = 20_000_000_000
OTHERS = ((EARLY, NEAR), (EARLY + NEAR, NEAR), (EARLY + 2 * NEAR, EARLY))


def other_kernel(square_ref, scale_ref, *refs):
    early_in, out_ref, result, sems = refs[:3], *refs[4:]
    stores = []
    for place, (start, width) in enumerate(OTHERS):
        cut = pl.ds(start - EARLY, width)
        result[:, cut] = both_steps_at_once(
            square_ref[...], scale_ref[:1, :1], early_in[place][...]
        )
        where = out_ref.at[:, pl.ds(start, width)]
        stores.append(pltpu.make_async_copy(result.at[:, cut], where, sems.at[place]))
        stores[-1].start()
    for store in stores:
        store.wait()


def early_products(polys, scale, early):
    out = jax.ShapeDtypeStruct((FF, SECOND), BF16)
    flops = 2 * FF * FF * EARLY
    result, square = pl.pallas_call(
        own_kernel,
        out_shape=(out, pltpu.HBM((FF, FF), BF16)),
        in_specs=[HBM, VMEM, HBM],
        out_specs=(HBM, HBM),
        scratch_shapes=[
            pltpu.VMEM((2, FF, FF), BF16),
            pltpu.VMEM((FF, EARLY), BF16),
            pltpu.VMEM((FF, FF), BF16),
            pltpu.VMEM((FF, EARLY), BF16),
            pltpu.SemaphoreType.DMA((5,)),
        ],
        cost_estimate=pl.CostEstimate(flops=7 * flops, bytes_accessed=0, transcendentals=0),
        compiler_params=LARGE,
    )(polys, scale, early[0])
    return pl.pallas_call(
        other_kernel,
        out_shape=out,
        in_specs=[VMEM] * 5 + [HBM],
        out_specs=HBM,
        scratch_shapes=[pltpu.VMEM((FF, SECOND - EARLY), BF16), pltpu.SemaphoreType.DMA((3,))],
        input_output_aliases={5: 0},
        cost_estimate=pl.CostEstimate(flops=ORDER, bytes_accessed=0, transcendentals=0),
        compiler_params=LARGE,
    )(square, scale, *early[1:], result)


def place_kernel(where, aliased, *refs):
    index = lax.axis_index("replica")
    chip, core = index // 2, index % 2
    count = len(where)
    pieces, out_ref, sems = refs[:count], refs[count + aliased], refs[count + aliased + 1]
    copies = []
    for number, (steps, cross, first, width, source) in enumerate(where):
        block = ((chip + steps) % 4) * 2 + (1 - core if cross else core)
        column = pl.multiple_of(block * WIDTH + first, 128)
        copies.append(
            pltpu.make_async_copy(
                pieces[number].at[:, :, pl.ds(source, width)],
                out_ref.at[:, :, pl.ds(column, width)],
                sems.at[number],
            )
        )
    for copy in copies:
        copy.start()
    for copy in copies:
        copy.wait()


def place(output, shape, pieces):
    arrays = [piece[0] for piece in pieces]
    where = tuple(piece[1:] for piece in pieces)
    aliased = output is not None
    anywhere = pl.BlockSpec(memory_space=pl.ANY)
    return pl.pallas_call(
        functools.partial(place_kernel, where, int(aliased)),
        out_shape=jax.ShapeDtypeStruct(shape, BF16),
        in_specs=[anywhere] * (len(arrays) + aliased),
        out_specs=anywhere,
        scratch_shapes=[pltpu.SemaphoreType.DMA((len(arrays),))],
        input_output_aliases={len(arrays): 0} if aliased else {},
        cost_estimate=pl.CostEstimate(flops=0, bytes_accessed=0, transcendentals=0),
        compiler_params=PARAMS,
    )(*arrays, *([output] if aliased else []))


def local(gradient, momentum):
    def stepped(gradient, momentum):
        return momentum_decay * momentum + gradient.astype(F32)

    ahead = gradient.astype(F32) + momentum_decay * stepped(gradient, momentum)
    experts, pairs, row_count, col_count = gradient.shape
    flat_rows = ahead.astype(BF16).reshape(experts * pairs, row_count, col_count)
    rows = lax.all_to_all(flat_rows, "tensor", split_axis=0, concat_axis=0, tiled=True)
    rows = rows.reshape(FF, col_count)

    keep, send, near, far = partial_gram(rows)
    own, to_next, to_last, to_far = chip_sum(keep, shift(send, 0, 1))
    mine = ring_sum(own, shift(to_next, 1), shift(to_last, -1), shift(to_far, 2))
    here = (mine, shift(mine, -1), shift(mine, 2), shift(mine, 1))
    other = tuple(shift(piece, 0, 1) for piece in here)
    late_rows, polys, scale = chain(here + other, rows)

    def back(value):
        value = value.reshape(experts * pairs, row_count, value.shape[1])
        return lax.all_to_all(value, "tensor", split_axis=0, concat_axis=0, tiled=True)

    gradient, momentum, late_rows = lax.optimization_barrier((gradient, momentum, late_rows))
    new_momentum = stepped(gradient, momentum)
    near, far, _ = lax.optimization_barrier((near, far, here[2]))
    early_rows = early_products(polys, scale, (far, shift(near, -1), shift(near, 1), shift(far, 2)))
    late = back(late_rows)
    late, early_rows, new_momentum = lax.optimization_barrier((late, early_rows, new_momentum))
    cut = late[:, :, :LATE]
    late_pieces = {0: late, 1: shift(cut, -1), 3: shift(cut, 1), 2: shift(late, 2)}
    widths = {0: FIRST, 1: LATE, 3: LATE, 2: FIRST}
    second = back(early_rows)

    shape = (experts * pairs, row_count, 8 * WIDTH)

    def late_place(pieces, steps, cross):
        return (pieces[steps], steps, cross, 0, widths[steps], 0)

    def early_places(value, cross, left, right):
        starts = {0: (0, EARLY), 1: OTHERS[0], 3: OTHERS[1], 2: OTHERS[2]}
        return [
            (value, steps, cross, WIDTH - width, width, start - left)
            for steps, (start, width) in starts.items()
            if left <= start < right
        ]

    late_across = {steps: shift(late_pieces[steps], 0, 1) for steps in (0, 1, 3)}
    places = [late_place(late_pieces, steps, 0) for steps in (0, 1, 3)]
    update = place(None, shape, places + [late_place(late_across, 0, 1)])
    late_pieces[2], update = lax.optimization_barrier((late_pieces[2], update))
    late_across[2] = shift(late_pieces[2], 0, 1)
    update = place(update, shape, [late_place(late_across, steps, 1) for steps in (1, 3)] + [late_place(late_pieces, 2, 0)])
    update = place(update, shape, [late_place(late_across, steps, 1) for steps in (2,)])
    second, update = lax.optimization_barrier((second, update))
    update = place(update, shape, early_places(second, 0, 0, SECOND))
    middle = EARLY + NEAR
    for left, right in ((0, middle), (middle, SECOND)):
        across = shift(second[:, :, left:right], 0, 1)
        update = place(update, shape, early_places(across, 1, left, right))
    return (update.reshape(experts, pairs, row_count, 8 * WIDTH), new_momentum)


def solution(mesh):
    in_specs = (P(None, None, "tensor", "replica"), P(None, None, "tensor", "replica"))
    out_specs = (P(None, None, "tensor", None), P(None, None, "tensor", "replica"))
    return jax.shard_map(local, mesh=mesh, in_specs=in_specs, out_specs=out_specs, check_vma=False)
```

```python
import functools
import math

import jax
import jax.numpy as jnp
from jax import lax
from jax.experimental import pallas as pl
from jax.experimental.pallas import tpu as pltpu
from jax.sharding import PartitionSpec as P

D = 4096
FF = 768

momentum_decay = 0.95
coef_linear = 3.4445
coef_gram = -4.775
coef_square = 2.0315
epsilon = 1e-07
scale_factor = 0.2 * math.sqrt(max(FF, D))

WIDTH = 512
LATE, MIDDLE, EARLY = 256, 0, 256
FIRST = LATE + MIDDLE
NEAR = MIDDLE + EARLY
SECOND = 2 * NEAR + 2 * EARLY
BLOCK = 256
HALF = FF
VMEM = pl.BlockSpec(memory_space=pltpu.VMEM)
HBM = pl.BlockSpec(memory_space=pltpu.HBM)
PARAMS = pltpu.CompilerParams(vmem_limit_bytes=16 * 1024 * 1024)
LARGE = pltpu.CompilerParams(vmem_limit_bytes=32 * 1024 * 1024)
F32, BF16 = jnp.float32, jnp.bfloat16


def replica_place():
    index = lax.axis_index("replica")
    return index // 2, index % 2


def shift(value, steps, cross=0):
    pairs = [
        (chip * 2 + core, ((chip + steps) % 4) * 2 + (core ^ cross))
        for chip in range(4)
        for core in range(2)
    ]
    return lax.ppermute(value, "replica", pairs)


def dot_t(left, right):
    return lax.dot_general(left, right, (((1,), (1,)), ((), ())), preferred_element_type=F32)


def dot(left, right):
    return jnp.dot(left, right, preferred_element_type=F32)


def gram_kernel(rows_ref, keep_ref, send_ref, near_ref, far_ref):
    core = lax.axis_index("replica") % 2

    def rows(index):
        return rows_ref[pl.ds(index * BLOCK, BLOCK), :]

    halves = (((0, 0), (1, 0), (1, 1)), ((2, 0), (2, 1), (2, 2)))
    for mine in range(2):

        @pl.when(core == mine)
        def _():
            for place in range(3):
                kept, sent = halves[mine][place], halves[1 - mine][place]
                where = pl.ds(place * BLOCK, BLOCK)
                keep_ref[where, :] = dot_t(rows(kept[0]), rows(kept[1]))
                send_ref[where, :] = dot_t(rows(sent[0]), rows(sent[1])).astype(BF16)

    near_ref[...] = rows_ref[:, LATE:]
    far_ref[...] = rows_ref[:, FIRST:]


def partial_gram(rows):
    return pl.pallas_call(
        gram_kernel,
        out_shape=(
            jax.ShapeDtypeStruct((HALF, BLOCK), F32),
            jax.ShapeDtypeStruct((HALF, BLOCK), BF16),
            jax.ShapeDtypeStruct((FF, NEAR), BF16),
            jax.ShapeDtypeStruct((FF, EARLY), BF16),
        ),
        in_specs=[VMEM],
        out_specs=(VMEM,) * 4,
        compiler_params=PARAMS,
    )(rows)


PIECE = HALF // 4


def chip_sum_kernel(keep_ref, got_ref, own_ref, next_ref, last_ref, far_ref):
    chip = lax.axis_index("replica") // 2

    def total(steps):
        where = pl.ds(pl.multiple_of(((chip + steps) % 4) * PIECE, PIECE), PIECE)
        return keep_ref[where, :] + got_ref[where, :].astype(F32)

    own_ref[...] = total(0)
    next_ref[...] = total(1).astype(BF16)
    last_ref[...] = total(3).astype(BF16)
    far_ref[...] = total(2).astype(BF16)


def chip_sum(keep, got):
    return pl.pallas_call(
        chip_sum_kernel,
        out_shape=(jax.ShapeDtypeStruct((PIECE, BLOCK), F32),)
        + (jax.ShapeDtypeStruct((PIECE, BLOCK), BF16),) * 3,
        in_specs=[VMEM, VMEM],
        out_specs=(VMEM,) * 4,
        compiler_params=PARAMS,
    )(keep, got)


def ring_sum_kernel(own_ref, a_ref, b_ref, c_ref, out_ref):
    total = own_ref[...] + a_ref[...].astype(F32) + b_ref[...].astype(F32) + c_ref[...].astype(F32)
    out_ref[...] = total.astype(BF16)


def ring_sum(own, first, second, third):
    return pl.pallas_call(
        ring_sum_kernel,
        out_shape=jax.ShapeDtypeStruct((PIECE, BLOCK), BF16),
        in_specs=[VMEM] * 4,
        out_specs=VMEM,
        compiler_params=PARAMS,
    )(own, first, second, third)


def chain_kernel(*refs):
    pieces, rows_ref = refs[:6], refs[6]
    out_ref, polys_out, scale_ref, packed, gram, polys, late, sems = refs[7:]
    index = lax.axis_index("replica")
    chip, core = index // 2, index % 2
    for steps in range(4):
        start = pl.multiple_of(((chip + steps) % 4) * PIECE, PIECE)
        packed[core, pl.ds(start, PIECE), :] = pieces[steps][...]
        if steps == 0:
            packed[1 - core, pl.ds(start, PIECE), :] = pieces[4][...]
        else:
            where = pl.ds((steps - 1) * PIECE, PIECE)
            packed[1 - core, pl.ds(start, PIECE), :] = pieces[5][where, :]
    row_id = lax.broadcasted_iota(jnp.int32, (BLOCK, BLOCK), 0)
    col_id = lax.broadcasted_iota(jnp.int32, (BLOCK, BLOCK), 1)
    diagonal = row_id == col_id
    places = ((0, 0), (1, 0), (1, 1), (2, 0), (2, 1), (2, 2))
    blocks = [packed[place // 3, pl.ds((place % 3) * BLOCK, BLOCK), :] for place in range(6)]
    squares = sum(
        jnp.sum(jnp.where(diagonal, block.astype(F32), 0.0))
        for block, (row, col) in zip(blocks, places)
        if row == col
    )
    squares = jnp.full((1, 1), squares, F32)
    scale = 1.0 / (jnp.sqrt(squares) + epsilon)
    for block, (row, col) in zip(blocks, places):
        scaled = (block.astype(F32) * scale) * scale
        gram[pl.ds(row * BLOCK, BLOCK), pl.ds(col * BLOCK, BLOCK)] = scaled.astype(BF16)
        if row != col:
            gram[pl.ds(col * BLOCK, BLOCK), pl.ds(row * BLOCK, BLOCK)] = scaled.T.astype(BF16)

    scale_ref[...] = jnp.broadcast_to(scale, scale_ref.shape)
    gram_0 = gram[...]
    poly_0 = (coef_gram * gram_0.astype(F32) + coef_square * dot(gram_0, gram_0)).astype(BF16)
    polys[0] = poly_0
    copies = [pltpu.make_async_copy(polys.at[0], polys_out.at[0], sems.at[0])]
    copies[0].start()
    rows = rows_ref[:, :FIRST]
    first = ((coef_linear * rows.astype(F32) + dot(poly_0, rows)) * scale).astype(BF16)
    half_way = (coef_linear * gram_0.astype(F32) + dot(poly_0, gram_0)).astype(BF16)
    gram_1 = (coef_linear * half_way.astype(F32) + dot(half_way, poly_0)).astype(BF16)
    for block in range(FF // BLOCK):
        where = pl.ds(block * BLOCK, BLOCK)
        cut = slice(block * BLOCK, (block + 1) * BLOCK)
        square = dot(gram_1[cut], gram_1)
        poly_1 = (coef_gram * gram_1[cut].astype(F32) + coef_square * square).astype(BF16)
        polys[1, where, :] = poly_1
        second = coef_linear * first[cut].astype(F32) + dot(poly_1, first)
        late[where, :] = (scale_factor * second).astype(BF16)
        for source, target, number in (
            (polys.at[1, where, :], polys_out.at[1, where, :], 1 + 2 * block),
            (late.at[where, :], out_ref.at[where, :], 2 + 2 * block),
        ):
            copies.append(pltpu.make_async_copy(source, target, sems.at[number]))
            copies[-1].start()
    for copy in copies:
        copy.wait()


def chain(pieces, rows):
    return pl.pallas_call(
        chain_kernel,
        out_shape=(
            jax.ShapeDtypeStruct((FF, FIRST), BF16),
            pltpu.HBM((2, FF, FF), BF16),
            jax.ShapeDtypeStruct((8, 128), F32),
        ),
        in_specs=[VMEM] * 7,
        out_specs=(HBM, HBM, VMEM),
        scratch_shapes=[
            pltpu.VMEM((2, HALF, BLOCK), BF16),
            pltpu.VMEM((FF, FF), BF16),
            pltpu.VMEM((2, FF, FF), BF16),
            pltpu.VMEM((FF, FIRST), BF16),
            pltpu.SemaphoreType.DMA((7,)),
        ],
        cost_estimate=pl.CostEstimate(flops=0, bytes_accessed=0, transcendentals=0),
        compiler_params=LARGE,
    )(*pieces, rows)


def both_steps_at_once(square, scale, rows):
    total = coef_linear * coef_linear * rows.astype(F32) + dot(square, rows)
    return ((scale_factor * scale) * total).astype(BF16)


def own_kernel(polys_ref, scale_ref, early_ref, out_ref, square_ref, result, sems):
    sums = polys_ref[0].astype(F32) + polys_ref[1].astype(F32)
    square_ref[...] = (coef_linear * sums + dot(polys_ref[1], polys_ref[0])).astype(BF16)
    result[...] = both_steps_at_once(square_ref[...], scale_ref[:1, :1], early_ref[...])
    store = pltpu.make_async_copy(result, out_ref.at[:, pl.ds(0, EARLY)], sems.at[0])
    store.start()
    store.wait()


ORDER = 20_000_000_000
OTHERS = ((EARLY, NEAR), (EARLY + NEAR, NEAR), (EARLY + 2 * NEAR, EARLY))


def other_kernel(square_ref, scale_ref, *refs):
    early_in, out_ref, result, sems = refs[:3], *refs[4:]
    stores = []
    for place, (start, width) in enumerate(OTHERS):
        cut = pl.ds(start - EARLY, width)
        result[:, cut] = both_steps_at_once(
            square_ref[...], scale_ref[:1, :1], early_in[place][...]
        )
        where = out_ref.at[:, pl.ds(start, width)]
        stores.append(pltpu.make_async_copy(result.at[:, cut], where, sems.at[place]))
        stores[-1].start()
    for store in stores:
        store.wait()


def early_products(polys, scale, early):
    out = jax.ShapeDtypeStruct((FF, SECOND), BF16)
    flops = 2 * FF * FF * EARLY
    result, square = pl.pallas_call(
        own_kernel,
        out_shape=(out, jax.ShapeDtypeStruct((FF, FF), BF16)),
        in_specs=[VMEM] * 3,
        out_specs=(HBM, VMEM),
        scratch_shapes=[pltpu.VMEM((FF, EARLY), BF16), pltpu.SemaphoreType.DMA((1,))],
        cost_estimate=pl.CostEstimate(flops=0, bytes_accessed=0, transcendentals=0),
        compiler_params=PARAMS,
    )(polys, scale, early[0])
    return pl.pallas_call(
        other_kernel,
        out_shape=out,
        in_specs=[VMEM] * 5 + [HBM],
        out_specs=HBM,
        scratch_shapes=[pltpu.VMEM((FF, SECOND - EARLY), BF16), pltpu.SemaphoreType.DMA((3,))],
        input_output_aliases={5: 0},
        cost_estimate=pl.CostEstimate(flops=ORDER, bytes_accessed=0, transcendentals=0),
        compiler_params=LARGE,
    )(square, scale, *early[1:], result)


def place_kernel(where, aliased, *refs):
    index = lax.axis_index("replica")
    chip, core = index // 2, index % 2
    count = len(where)
    pieces, out_ref, sems = refs[:count], refs[count + aliased], refs[count + aliased + 1]
    copies = []
    for number, (steps, cross, first, width, source) in enumerate(where):
        block = ((chip + steps) % 4) * 2 + (1 - core if cross else core)
        column = pl.multiple_of(block * WIDTH + first, 128)
        copies.append(
            pltpu.make_async_copy(
                pieces[number].at[:, :, pl.ds(source, width)],
                out_ref.at[:, :, pl.ds(column, width)],
                sems.at[number],
            )
        )
    for copy in copies:
        copy.start()
    for copy in copies:
        copy.wait()


def place(output, shape, pieces):
    arrays = [piece[0] for piece in pieces]
    where = tuple(piece[1:] for piece in pieces)
    aliased = output is not None
    anywhere = pl.BlockSpec(memory_space=pl.ANY)
    return pl.pallas_call(
        functools.partial(place_kernel, where, int(aliased)),
        out_shape=jax.ShapeDtypeStruct(shape, BF16),
        in_specs=[VMEM] * len(arrays) + [anywhere] * aliased,
        out_specs=anywhere,
        scratch_shapes=[pltpu.SemaphoreType.DMA((len(arrays),))],
        input_output_aliases={len(arrays): 0} if aliased else {},
        cost_estimate=pl.CostEstimate(flops=0, bytes_accessed=0, transcendentals=0),
        compiler_params=PARAMS,
    )(*arrays, *([output] if aliased else []))


def local(gradient, momentum):
    def stepped(gradient, momentum):
        return momentum_decay * momentum + gradient.astype(F32)

    ahead = gradient.astype(F32) + momentum_decay * stepped(gradient, momentum)
    experts, pairs, row_count, col_count = gradient.shape
    flat_rows = ahead.astype(BF16).reshape(experts * pairs, row_count, col_count)
    rows = lax.all_to_all(flat_rows, "tensor", split_axis=0, concat_axis=0, tiled=True)
    rows = rows.reshape(FF, col_count)

    keep, send, near, far = partial_gram(rows)
    own, to_next, to_last, to_far = chip_sum(keep, shift(send, 0, 1))
    mine = ring_sum(own, shift(to_next, 1), shift(to_last, -1), shift(to_far, 2))
    here = (mine, shift(mine, -1), shift(mine, 2), shift(mine, 1))
    other = shift(jnp.concatenate(here[1:]), 0, 1)
    late_rows, polys, scale = chain((*here, shift(mine, 0, 1), other), rows)

    def back(value):
        value = value.reshape(experts * pairs, row_count, value.shape[1])
        return lax.all_to_all(value, "tensor", split_axis=0, concat_axis=0, tiled=True)

    near, far, _ = lax.optimization_barrier((near, far, here[2]))
    early_rows = early_products(polys, scale, (far, shift(near, -1), shift(near, 1), shift(far, 2)))
    late = back(late_rows)
    late, early_rows = lax.optimization_barrier((late, early_rows))
    gradient, momentum, _ = lax.optimization_barrier((gradient, momentum, late))
    new_momentum = stepped(gradient, momentum)
    cut = late[:, :, :LATE]
    late_pieces = {0: late, 1: shift(cut, -1), 3: shift(cut, 1), 2: shift(late, 2)}
    widths = {0: FIRST, 1: LATE, 3: LATE, 2: FIRST}
    second = back(early_rows)

    shape = (experts * pairs, row_count, 8 * WIDTH)

    def late_place(pieces, steps, cross):
        return (pieces[steps], steps, cross, 0, widths[steps], 0)

    def early_places(value, cross, left, right):
        starts = {0: (0, EARLY), 1: OTHERS[0], 3: OTHERS[1], 2: OTHERS[2]}
        return [
            (value, steps, cross, WIDTH - width, width, start - left)
            for steps, (start, width) in starts.items()
            if left <= start < right
        ]

    late_across = {steps: shift(late_pieces[steps], 0, 1) for steps in (0, 1, 3)}
    places = [late_place(late_pieces, steps, 0) for steps in (0, 1, 3)]
    update = place(None, shape, places + [late_place(late_across, 0, 1)])
    late_pieces[2], update = lax.optimization_barrier((late_pieces[2], update))
    late_across[2] = shift(late_pieces[2], 0, 1)
    update = place(update, shape, [late_place(late_across, steps, 1) for steps in (1, 3)] + [late_place(late_pieces, 2, 0)])
    update = place(update, shape, [late_place(late_across, steps, 1) for steps in (2,)])
    second, update, new_momentum = lax.optimization_barrier((second, update, new_momentum))
    update = place(update, shape, early_places(second, 0, 0, SECOND))
    middle = EARLY + NEAR
    for left, right in ((0, middle), (middle, SECOND)):
        across = shift(second[:, :, left:right], 0, 1)
        update = place(update, shape, early_places(across, 1, left, right))
    return (update.reshape(experts, pairs, row_count, 8 * WIDTH), new_momentum)


def solution(mesh):
    in_specs = (P(None, None, "tensor", "replica"), P(None, None, "tensor", "replica"))
    out_specs = (P(None, None, "tensor", None), P(None, None, "tensor", "replica"))
    return jax.shard_map(local, mesh=mesh, in_specs=in_specs, out_specs=out_specs, check_vma=False)
```

```python
import functools
import math

import jax
import jax.numpy as jnp
from jax import lax
from jax.experimental import pallas as pl
from jax.experimental.pallas import tpu as pltpu
from jax.sharding import PartitionSpec as P

D = 4096
FF = 768

momentum_decay = 0.95
coef_linear = 3.4445
coef_gram = -4.775
coef_square = 2.0315
epsilon = 1e-07
scale_factor = 0.2 * math.sqrt(max(FF, D))

WIDTH = 512
LATE, MIDDLE, EARLY = 256, 0, 256
FIRST = LATE + MIDDLE
NEAR = MIDDLE + EARLY
SECOND = 2 * NEAR + 2 * EARLY
BLOCK = 256
HALF = FF
VMEM = pl.BlockSpec(memory_space=pltpu.VMEM)
HBM = pl.BlockSpec(memory_space=pltpu.HBM)
PARAMS = pltpu.CompilerParams(vmem_limit_bytes=16 * 1024 * 1024)
LARGE = pltpu.CompilerParams(vmem_limit_bytes=32 * 1024 * 1024)
F32, BF16 = jnp.float32, jnp.bfloat16


def replica_place():
    index = lax.axis_index("replica")
    return index // 2, index % 2


def shift(value, steps, cross=0):
    pairs = [
        (chip * 2 + core, ((chip + steps) % 4) * 2 + (core ^ cross))
        for chip in range(4)
        for core in range(2)
    ]
    return lax.ppermute(value, "replica", pairs)


def dot_t(left, right):
    return lax.dot_general(left, right, (((1,), (1,)), ((), ())), preferred_element_type=F32)


def dot(left, right):
    return jnp.dot(left, right, preferred_element_type=F32)


def gram_kernel(rows_ref, keep_ref, send_ref, near_ref, far_ref):
    core = lax.axis_index("replica") % 2

    def rows(index):
        return rows_ref[pl.ds(index * BLOCK, BLOCK), :]

    halves = (((0, 0), (1, 0), (1, 1)), ((2, 0), (2, 1), (2, 2)))
    for mine in range(2):

        @pl.when(core == mine)
        def _():
            for place in range(3):
                kept, sent = halves[mine][place], halves[1 - mine][place]
                where = pl.ds(place * BLOCK, BLOCK)
                keep_ref[where, :] = dot_t(rows(kept[0]), rows(kept[1]))
                send_ref[where, :] = dot_t(rows(sent[0]), rows(sent[1])).astype(BF16)

    near_ref[...] = rows_ref[:, LATE:]
    far_ref[...] = rows_ref[:, FIRST:]


def partial_gram(rows):
    return pl.pallas_call(
        gram_kernel,
        out_shape=(
            jax.ShapeDtypeStruct((HALF, BLOCK), F32),
            jax.ShapeDtypeStruct((HALF, BLOCK), BF16),
            jax.ShapeDtypeStruct((FF, NEAR), BF16),
            jax.ShapeDtypeStruct((FF, EARLY), BF16),
        ),
        in_specs=[VMEM],
        out_specs=(VMEM,) * 4,
        compiler_params=PARAMS,
    )(rows)


PIECE = HALF // 4


def chip_sum_kernel(keep_ref, got_ref, own_ref, next_ref, last_ref, far_ref):
    chip = lax.axis_index("replica") // 2

    def total(steps):
        where = pl.ds(pl.multiple_of(((chip + steps) % 4) * PIECE, PIECE), PIECE)
        return keep_ref[where, :] + got_ref[where, :].astype(F32)

    own_ref[...] = total(0)
    next_ref[...] = total(1).astype(BF16)
    last_ref[...] = total(3).astype(BF16)
    far_ref[...] = total(2).astype(BF16)


def chip_sum(keep, got):
    return pl.pallas_call(
        chip_sum_kernel,
        out_shape=(jax.ShapeDtypeStruct((PIECE, BLOCK), F32),)
        + (jax.ShapeDtypeStruct((PIECE, BLOCK), BF16),) * 3,
        in_specs=[VMEM, VMEM],
        out_specs=(VMEM,) * 4,
        compiler_params=PARAMS,
    )(keep, got)


def ring_sum_kernel(own_ref, a_ref, b_ref, c_ref, out_ref):
    total = own_ref[...] + a_ref[...].astype(F32) + b_ref[...].astype(F32) + c_ref[...].astype(F32)
    out_ref[...] = total.astype(BF16)


def ring_sum(own, first, second, third):
    return pl.pallas_call(
        ring_sum_kernel,
        out_shape=jax.ShapeDtypeStruct((PIECE, BLOCK), BF16),
        in_specs=[VMEM] * 4,
        out_specs=VMEM,
        compiler_params=PARAMS,
    )(own, first, second, third)


def chain_kernel(*refs):
    pieces, rows_ref = refs[:6], refs[6]
    out_ref, polys_out, scale_ref, packed, gram, polys, late, sems = refs[7:]
    index = lax.axis_index("replica")
    chip, core = index // 2, index % 2
    for steps in range(4):
        start = pl.multiple_of(((chip + steps) % 4) * PIECE, PIECE)
        packed[core, pl.ds(start, PIECE), :] = pieces[steps][...]
        if steps == 0:
            packed[1 - core, pl.ds(start, PIECE), :] = pieces[4][...]
        else:
            where = pl.ds((steps - 1) * PIECE, PIECE)
            packed[1 - core, pl.ds(start, PIECE), :] = pieces[5][where, :]
    row_id = lax.broadcasted_iota(jnp.int32, (BLOCK, BLOCK), 0)
    col_id = lax.broadcasted_iota(jnp.int32, (BLOCK, BLOCK), 1)
    diagonal = row_id == col_id
    places = ((0, 0), (1, 0), (1, 1), (2, 0), (2, 1), (2, 2))
    blocks = [packed[place // 3, pl.ds((place % 3) * BLOCK, BLOCK), :] for place in range(6)]
    squares = sum(
        jnp.sum(jnp.where(diagonal, block.astype(F32), 0.0))
        for block, (row, col) in zip(blocks, places)
        if row == col
    )
    squares = jnp.full((1, 1), squares, F32)
    scale = 1.0 / (jnp.sqrt(squares) + epsilon)
    for block, (row, col) in zip(blocks, places):
        scaled = (block.astype(F32) * scale) * scale
        gram[pl.ds(row * BLOCK, BLOCK), pl.ds(col * BLOCK, BLOCK)] = scaled.astype(BF16)
        if row != col:
            gram[pl.ds(col * BLOCK, BLOCK), pl.ds(row * BLOCK, BLOCK)] = scaled.T.astype(BF16)

    scale_ref[...] = jnp.broadcast_to(scale, scale_ref.shape)
    gram_0 = gram[...]
    poly_0 = (coef_gram * gram_0.astype(F32) + coef_square * dot(gram_0, gram_0)).astype(BF16)
    polys[0] = poly_0
    copies = [pltpu.make_async_copy(polys.at[0], polys_out.at[0], sems.at[0])]
    copies[0].start()
    rows = rows_ref[:, :FIRST]
    first = ((coef_linear * rows.astype(F32) + dot(poly_0, rows)) * scale).astype(BF16)
    half_way = (coef_linear * gram_0.astype(F32) + dot(poly_0, gram_0)).astype(BF16)
    gram_1 = (coef_linear * half_way.astype(F32) + dot(half_way, poly_0)).astype(BF16)
    for block in range(FF // BLOCK):
        where = pl.ds(block * BLOCK, BLOCK)
        cut = slice(block * BLOCK, (block + 1) * BLOCK)
        square = dot(gram_1[cut], gram_1)
        poly_1 = (coef_gram * gram_1[cut].astype(F32) + coef_square * square).astype(BF16)
        polys[1, where, :] = poly_1
        second = coef_linear * first[cut].astype(F32) + dot(poly_1, first)
        late[where, :] = (scale_factor * second).astype(BF16)
        for source, target, number in (
            (polys.at[1, where, :], polys_out.at[1, where, :], 1 + 2 * block),
            (late.at[where, :], out_ref.at[where, :], 2 + 2 * block),
        ):
            copies.append(pltpu.make_async_copy(source, target, sems.at[number]))
            copies[-1].start()
    for copy in copies:
        copy.wait()


def chain(pieces, rows):
    return pl.pallas_call(
        chain_kernel,
        out_shape=(
            jax.ShapeDtypeStruct((FF, FIRST), BF16),
            pltpu.HBM((2, FF, FF), BF16),
            jax.ShapeDtypeStruct((8, 128), F32),
        ),
        in_specs=[VMEM] * 7,
        out_specs=(HBM, HBM, VMEM),
        scratch_shapes=[
            pltpu.VMEM((2, HALF, BLOCK), BF16),
            pltpu.VMEM((FF, FF), BF16),
            pltpu.VMEM((2, FF, FF), BF16),
            pltpu.VMEM((FF, FIRST), BF16),
            pltpu.SemaphoreType.DMA((7,)),
        ],
        cost_estimate=pl.CostEstimate(flops=0, bytes_accessed=0, transcendentals=0),
        compiler_params=LARGE,
    )(*pieces, rows)


def both_steps(poly_0, poly_1, scale, rows):
    first = ((coef_linear * rows.astype(F32) + dot(poly_0, rows)) * scale).astype(BF16)
    second = coef_linear * first.astype(F32) + dot(poly_1, first)
    return (scale_factor * second).astype(BF16)


def own_kernel(polys_ref, scale_ref, early_ref, out_ref, result, sems):
    result[...] = both_steps(polys_ref[0], polys_ref[1], scale_ref[:1, :1], early_ref[...])
    store = pltpu.make_async_copy(result, out_ref.at[:, pl.ds(0, EARLY)], sems.at[0])
    store.start()
    store.wait()


ORDER = 20_000_000_000
OTHERS = ((EARLY, NEAR), (EARLY + NEAR, NEAR), (EARLY + 2 * NEAR, EARLY))


def other_kernel(polys_ref, scale_ref, *refs):
    early_in, out_ref, early, result, sems = refs[:3], *refs[4:]
    for place, (start, width) in enumerate(OTHERS):
        early[:, pl.ds(start - EARLY, width)] = early_in[place][...]
    rows = early[...]
    total = coef_linear * rows.astype(F32) + dot(polys_ref[0], rows)
    first = (total * scale_ref[:1, :1]).astype(BF16)
    stores = []
    for block in range(FF // BLOCK):
        where = pl.ds(block * BLOCK, BLOCK)
        cut = slice(block * BLOCK, (block + 1) * BLOCK)
        second = coef_linear * first[cut].astype(F32) + dot(polys_ref[1, where, :], first)
        result[where, :] = (scale_factor * second).astype(BF16)
        target = out_ref.at[where, pl.ds(EARLY, SECOND - EARLY)]
        stores.append(pltpu.make_async_copy(result.at[where, :], target, sems.at[block]))
        stores[-1].start()
    for store in stores:
        store.wait()


def early_products(polys, scale, early):
    out = jax.ShapeDtypeStruct((FF, SECOND), BF16)
    flops = 2 * FF * FF * EARLY
    result = pl.pallas_call(
        own_kernel,
        out_shape=out,
        in_specs=[VMEM] * 3,
        out_specs=HBM,
        scratch_shapes=[pltpu.VMEM((FF, EARLY), BF16), pltpu.SemaphoreType.DMA((1,))],
        cost_estimate=pl.CostEstimate(flops=0, bytes_accessed=0, transcendentals=0),
        compiler_params=PARAMS,
    )(polys, scale, early[0])
    return pl.pallas_call(
        other_kernel,
        out_shape=out,
        in_specs=[VMEM] * 5 + [HBM],
        out_specs=HBM,
        scratch_shapes=[
            pltpu.VMEM((FF, SECOND - EARLY), BF16),
            pltpu.VMEM((FF, SECOND - EARLY), BF16),
            pltpu.SemaphoreType.DMA((3,)),
        ],
        input_output_aliases={5: 0},
        cost_estimate=pl.CostEstimate(flops=ORDER, bytes_accessed=0, transcendentals=0),
        compiler_params=LARGE,
    )(polys, scale, *early[1:], result)


def place_kernel(where, aliased, *refs):
    index = lax.axis_index("replica")
    chip, core = index // 2, index % 2
    count = len(where)
    pieces, out_ref, sems = refs[:count], refs[count + aliased], refs[count + aliased + 1]
    copies = []
    for number, (steps, cross, first, width, source) in enumerate(where):
        block = ((chip + steps) % 4) * 2 + (1 - core if cross else core)
        column = pl.multiple_of(block * WIDTH + first, 128)
        copies.append(
            pltpu.make_async_copy(
                pieces[number].at[:, :, pl.ds(source, width)],
                out_ref.at[:, :, pl.ds(column, width)],
                sems.at[number],
            )
        )
    for copy in copies:
        copy.start()
    for copy in copies:
        copy.wait()


def place(output, shape, pieces):
    arrays = [piece[0] for piece in pieces]
    where = tuple(piece[1:] for piece in pieces)
    aliased = output is not None
    anywhere = pl.BlockSpec(memory_space=pl.ANY)
    return pl.pallas_call(
        functools.partial(place_kernel, where, int(aliased)),
        out_shape=jax.ShapeDtypeStruct(shape, BF16),
        in_specs=[VMEM] * len(arrays) + [anywhere] * aliased,
        out_specs=anywhere,
        scratch_shapes=[pltpu.SemaphoreType.DMA((len(arrays),))],
        input_output_aliases={len(arrays): 0} if aliased else {},
        cost_estimate=pl.CostEstimate(flops=0, bytes_accessed=0, transcendentals=0),
        compiler_params=PARAMS,
    )(*arrays, *([output] if aliased else []))


def local(gradient, momentum):
    def stepped(gradient, momentum):
        return momentum_decay * momentum + gradient.astype(F32)

    ahead = gradient.astype(F32) + momentum_decay * stepped(gradient, momentum)
    experts, pairs, row_count, col_count = gradient.shape
    flat_rows = ahead.astype(BF16).reshape(experts * pairs, row_count, col_count)
    rows = lax.all_to_all(flat_rows, "tensor", split_axis=0, concat_axis=0, tiled=True)
    rows = rows.reshape(FF, col_count)

    keep, send, near, far = partial_gram(rows)
    own, to_next, to_last, to_far = chip_sum(keep, shift(send, 0, 1))
    gradient, momentum, own = lax.optimization_barrier((gradient, momentum, own))
    new_momentum = stepped(gradient, momentum)
    own, new_momentum = lax.optimization_barrier((own, new_momentum))
    mine = ring_sum(own, shift(to_next, 1), shift(to_last, -1), shift(to_far, 2))
    here = (mine, shift(mine, -1), shift(mine, 2), shift(mine, 1))
    other = shift(jnp.concatenate(here[1:]), 0, 1)
    late_rows, polys, scale = chain((*here, shift(mine, 0, 1), other), rows)

    def back(value):
        value = value.reshape(experts * pairs, row_count, value.shape[1])
        return lax.all_to_all(value, "tensor", split_axis=0, concat_axis=0, tiled=True)

    near, far, _ = lax.optimization_barrier((near, far, here[2]))
    early_rows = early_products(polys, scale, (far, shift(near, -1), shift(near, 1), shift(far, 2)))
    late = back(late_rows)
    late, early_rows = lax.optimization_barrier((late, early_rows))
    cut = late[:, :, :LATE]
    late_pieces = {0: late, 1: shift(cut, -1), 3: shift(cut, 1), 2: shift(late, 2)}
    widths = {0: FIRST, 1: LATE, 3: LATE, 2: FIRST}
    second = back(early_rows)

    shape = (experts * pairs, row_count, 8 * WIDTH)

    def late_place(pieces, steps, cross):
        return (pieces[steps], steps, cross, 0, widths[steps], 0)

    def early_places(value, cross, left, right):
        starts = {0: (0, EARLY), 1: OTHERS[0], 3: OTHERS[1], 2: OTHERS[2]}
        return [
            (value, steps, cross, WIDTH - width, width, start - left)
            for steps, (start, width) in starts.items()
            if left <= start < right
        ]

    late_across = {steps: shift(late_pieces[steps], 0, 1) for steps in (0, 1, 3)}
    places = [late_place(late_pieces, steps, 0) for steps in (0, 1, 3)]
    update = place(None, shape, places + [late_place(late_across, 0, 1)])
    late_pieces[2], update = lax.optimization_barrier((late_pieces[2], update))
    late_across[2] = shift(late_pieces[2], 0, 1)
    update = place(update, shape, [late_place(late_across, steps, 1) for steps in (1, 3)] + [late_place(late_pieces, 2, 0)])
    update = place(update, shape, [late_place(late_across, steps, 1) for steps in (2,)])
    second, update = lax.optimization_barrier((second, update))
    update = place(update, shape, early_places(second, 0, 0, SECOND))
    middle = EARLY + NEAR
    for left, right in ((0, middle), (middle, SECOND)):
        across = shift(second[:, :, left:right], 0, 1)
        update = place(update, shape, early_places(across, 1, left, right))
    return (update.reshape(experts, pairs, row_count, 8 * WIDTH), new_momentum)


def solution(mesh):
    in_specs = (P(None, None, "tensor", "replica"), P(None, None, "tensor", "replica"))
    out_specs = (P(None, None, "tensor", None), P(None, None, "tensor", "replica"))
    return jax.shard_map(local, mesh=mesh, in_specs=in_specs, out_specs=out_specs, check_vma=False)
```

```python
import functools
import math

import jax
import jax.numpy as jnp
from jax import lax
from jax.experimental import pallas as pl
from jax.experimental.pallas import tpu as pltpu
from jax.sharding import PartitionSpec as P

D = 4096
FF = 768

momentum_decay = 0.95
coef_linear = 3.4445
coef_gram = -4.775
coef_square = 2.0315
epsilon = 1e-07
scale_factor = 0.2 * math.sqrt(max(FF, D))

WIDTH = 512
LATE, MIDDLE, EARLY = 256, 0, 256
FIRST = LATE + MIDDLE
NEAR = MIDDLE + EARLY
SECOND = 2 * NEAR + 2 * EARLY
BLOCK = 256
HALF = FF
VMEM = pl.BlockSpec(memory_space=pltpu.VMEM)
HBM = pl.BlockSpec(memory_space=pltpu.HBM)
PARAMS = pltpu.CompilerParams(vmem_limit_bytes=16 * 1024 * 1024)
LARGE = pltpu.CompilerParams(vmem_limit_bytes=32 * 1024 * 1024)
F32, BF16 = jnp.float32, jnp.bfloat16


def replica_place():
    index = lax.axis_index("replica")
    return index // 2, index % 2


def shift(value, steps, cross=0):
    pairs = [
        (chip * 2 + core, ((chip + steps) % 4) * 2 + (core ^ cross))
        for chip in range(4)
        for core in range(2)
    ]
    return lax.ppermute(value, "replica", pairs)


def dot_t(left, right):
    return lax.dot_general(left, right, (((1,), (1,)), ((), ())), preferred_element_type=F32)


def dot(left, right):
    return jnp.dot(left, right, preferred_element_type=F32)


def gram_kernel(rows_ref, keep_ref, send_ref, near_ref, far_ref):
    core = lax.axis_index("replica") % 2

    def rows(index):
        return rows_ref[pl.ds(index * BLOCK, BLOCK), :]

    halves = (((0, 0), (1, 0), (1, 1)), ((2, 0), (2, 1), (2, 2)))
    for mine in range(2):

        @pl.when(core == mine)
        def _():
            for place in range(3):
                kept, sent = halves[mine][place], halves[1 - mine][place]
                where = pl.ds(place * BLOCK, BLOCK)
                keep_ref[where, :] = dot_t(rows(kept[0]), rows(kept[1]))
                send_ref[where, :] = dot_t(rows(sent[0]), rows(sent[1])).astype(BF16)

    near_ref[...] = rows_ref[:, LATE:]
    far_ref[...] = rows_ref[:, FIRST:]


def partial_gram(rows):
    return pl.pallas_call(
        gram_kernel,
        out_shape=(
            jax.ShapeDtypeStruct((HALF, BLOCK), F32),
            jax.ShapeDtypeStruct((HALF, BLOCK), BF16),
            jax.ShapeDtypeStruct((FF, NEAR), BF16),
            jax.ShapeDtypeStruct((FF, EARLY), BF16),
        ),
        in_specs=[VMEM],
        out_specs=(VMEM,) * 4,
        compiler_params=PARAMS,
    )(rows)


PIECE = HALF // 4


def chip_sum_kernel(keep_ref, got_ref, own_ref, next_ref, last_ref, far_ref):
    chip = lax.axis_index("replica") // 2

    def total(steps):
        where = pl.ds(pl.multiple_of(((chip + steps) % 4) * PIECE, PIECE), PIECE)
        return keep_ref[where, :] + got_ref[where, :].astype(F32)

    own_ref[...] = total(0)
    next_ref[...] = total(1).astype(BF16)
    last_ref[...] = total(3).astype(BF16)
    far_ref[...] = total(2).astype(BF16)


def chip_sum(keep, got):
    return pl.pallas_call(
        chip_sum_kernel,
        out_shape=(jax.ShapeDtypeStruct((PIECE, BLOCK), F32),)
        + (jax.ShapeDtypeStruct((PIECE, BLOCK), BF16),) * 3,
        in_specs=[VMEM, VMEM],
        out_specs=(VMEM,) * 4,
        compiler_params=PARAMS,
    )(keep, got)


def ring_sum_kernel(own_ref, a_ref, b_ref, c_ref, out_ref):
    total = own_ref[...] + a_ref[...].astype(F32) + b_ref[...].astype(F32) + c_ref[...].astype(F32)
    out_ref[...] = total.astype(BF16)


def ring_sum(own, first, second, third):
    return pl.pallas_call(
        ring_sum_kernel,
        out_shape=jax.ShapeDtypeStruct((PIECE, BLOCK), BF16),
        in_specs=[VMEM] * 4,
        out_specs=VMEM,
        compiler_params=PARAMS,
    )(own, first, second, third)


def chain_kernel(*refs):
    pieces, rows_ref = refs[:6], refs[6]
    out_ref, polys_out, scale_ref, packed, gram, polys, late, sems = refs[7:]
    index = lax.axis_index("replica")
    chip, core = index // 2, index % 2
    for steps in range(4):
        start = pl.multiple_of(((chip + steps) % 4) * PIECE, PIECE)
        packed[core, pl.ds(start, PIECE), :] = pieces[steps][...]
        if steps == 0:
            packed[1 - core, pl.ds(start, PIECE), :] = pieces[4][...]
        else:
            where = pl.ds((steps - 1) * PIECE, PIECE)
            packed[1 - core, pl.ds(start, PIECE), :] = pieces[5][where, :]
    row_id = lax.broadcasted_iota(jnp.int32, (BLOCK, BLOCK), 0)
    col_id = lax.broadcasted_iota(jnp.int32, (BLOCK, BLOCK), 1)
    diagonal = row_id == col_id
    places = ((0, 0), (1, 0), (1, 1), (2, 0), (2, 1), (2, 2))
    blocks = [packed[place // 3, pl.ds((place % 3) * BLOCK, BLOCK), :] for place in range(6)]
    squares = sum(
        jnp.sum(jnp.where(diagonal, block.astype(F32), 0.0))
        for block, (row, col) in zip(blocks, places)
        if row == col
    )
    squares = jnp.full((1, 1), squares, F32)
    scale = 1.0 / (jnp.sqrt(squares) + epsilon)
    for block, (row, col) in zip(blocks, places):
        scaled = (block.astype(F32) * scale) * scale
        gram[pl.ds(row * BLOCK, BLOCK), pl.ds(col * BLOCK, BLOCK)] = scaled.astype(BF16)
        if row != col:
            gram[pl.ds(col * BLOCK, BLOCK), pl.ds(row * BLOCK, BLOCK)] = scaled.T.astype(BF16)

    scale_ref[...] = jnp.broadcast_to(scale, scale_ref.shape)
    gram_0 = gram[...]
    poly_0 = (coef_gram * gram_0.astype(F32) + coef_square * dot(gram_0, gram_0)).astype(BF16)
    polys[0] = poly_0
    copies = [pltpu.make_async_copy(polys.at[0], polys_out.at[0], sems.at[0])]
    copies[0].start()
    rows = rows_ref[:, :FIRST]
    first = ((coef_linear * rows.astype(F32) + dot(poly_0, rows)) * scale).astype(BF16)
    half_way = (coef_linear * gram_0.astype(F32) + dot(poly_0, gram_0)).astype(BF16)
    gram_1 = (coef_linear * half_way.astype(F32) + dot(half_way, poly_0)).astype(BF16)
    for block in range(FF // BLOCK):
        where = pl.ds(block * BLOCK, BLOCK)
        cut = slice(block * BLOCK, (block + 1) * BLOCK)
        square = dot(gram_1[cut], gram_1)
        poly_1 = (coef_gram * gram_1[cut].astype(F32) + coef_square * square).astype(BF16)
        polys[1, where, :] = poly_1
        second = coef_linear * first[cut].astype(F32) + dot(poly_1, first)
        late[where, :] = (scale_factor * second).astype(BF16)
        for source, target, number in (
            (polys.at[1, where, :], polys_out.at[1, where, :], 1 + 2 * block),
            (late.at[where, :], out_ref.at[where, :], 2 + 2 * block),
        ):
            copies.append(pltpu.make_async_copy(source, target, sems.at[number]))
            copies[-1].start()
    for copy in copies:
        copy.wait()


def chain(pieces, rows):
    return pl.pallas_call(
        chain_kernel,
        out_shape=(
            jax.ShapeDtypeStruct((FF, FIRST), BF16),
            pltpu.HBM((2, FF, FF), BF16),
            jax.ShapeDtypeStruct((8, 128), F32),
        ),
        in_specs=[VMEM] * 7,
        out_specs=(HBM, HBM, VMEM),
        scratch_shapes=[
            pltpu.VMEM((2, HALF, BLOCK), BF16),
            pltpu.VMEM((FF, FF), BF16),
            pltpu.VMEM((2, FF, FF), BF16),
            pltpu.VMEM((FF, FIRST), BF16),
            pltpu.SemaphoreType.DMA((7,)),
        ],
        cost_estimate=pl.CostEstimate(flops=0, bytes_accessed=0, transcendentals=0),
        compiler_params=LARGE,
    )(*pieces, rows)


def both_steps(poly_0, poly_1, scale, rows):
    first = ((coef_linear * rows.astype(F32) + dot(poly_0, rows)) * scale).astype(BF16)
    second = coef_linear * first.astype(F32) + dot(poly_1, first)
    return (scale_factor * second).astype(BF16)


def own_kernel(polys_ref, scale_ref, early_ref, out_ref, result, sems):
    result[...] = both_steps(polys_ref[0], polys_ref[1], scale_ref[:1, :1], early_ref[...])
    store = pltpu.make_async_copy(result, out_ref.at[:, pl.ds(0, EARLY)], sems.at[0])
    store.start()
    store.wait()


ORDER = 20_000_000_000
OTHERS = ((EARLY, NEAR), (EARLY + NEAR, NEAR), (EARLY + 2 * NEAR, EARLY))


def other_kernel(polys_ref, scale_ref, *refs):
    early_in, out_ref, early, result, sems = refs[:3], *refs[4:]
    for place, (start, width) in enumerate(OTHERS):
        early[:, pl.ds(start - EARLY, width)] = early_in[place][...]
    rows = early[...]
    total = coef_linear * rows.astype(F32) + dot(polys_ref[0], rows)
    first = (total * scale_ref[:1, :1]).astype(BF16)
    stores = []
    for block in range(FF // BLOCK):
        where = pl.ds(block * BLOCK, BLOCK)
        cut = slice(block * BLOCK, (block + 1) * BLOCK)
        second = coef_linear * first[cut].astype(F32) + dot(polys_ref[1, where, :], first)
        result[where, :] = (scale_factor * second).astype(BF16)
        target = out_ref.at[where, pl.ds(EARLY, SECOND - EARLY)]
        stores.append(pltpu.make_async_copy(result.at[where, :], target, sems.at[block]))
        stores[-1].start()
    for store in stores:
        store.wait()


def early_products(polys, scale, early):
    out = jax.ShapeDtypeStruct((FF, SECOND), BF16)
    flops = 2 * FF * FF * EARLY
    result = pl.pallas_call(
        own_kernel,
        out_shape=out,
        in_specs=[VMEM] * 3,
        out_specs=HBM,
        scratch_shapes=[pltpu.VMEM((FF, EARLY), BF16), pltpu.SemaphoreType.DMA((1,))],
        cost_estimate=pl.CostEstimate(flops=0, bytes_accessed=0, transcendentals=0),
        compiler_params=PARAMS,
    )(polys, scale, early[0])
    return pl.pallas_call(
        other_kernel,
        out_shape=out,
        in_specs=[VMEM] * 5 + [HBM],
        out_specs=HBM,
        scratch_shapes=[
            pltpu.VMEM((FF, SECOND - EARLY), BF16),
            pltpu.VMEM((FF, SECOND - EARLY), BF16),
            pltpu.SemaphoreType.DMA((3,)),
        ],
        input_output_aliases={5: 0},
        cost_estimate=pl.CostEstimate(flops=ORDER, bytes_accessed=0, transcendentals=0),
        compiler_params=LARGE,
    )(polys, scale, *early[1:], result)


def place_kernel(where, aliased, *refs):
    index = lax.axis_index("replica")
    chip, core = index // 2, index % 2
    count = len(where)
    pieces, out_ref, sems = refs[:count], refs[count + aliased], refs[count + aliased + 1]
    copies = []
    for number, (steps, cross, first, width, source) in enumerate(where):
        block = ((chip + steps) % 4) * 2 + (1 - core if cross else core)
        column = pl.multiple_of(block * WIDTH + first, 128)
        copies.append(
            pltpu.make_async_copy(
                pieces[number].at[:, :, pl.ds(source, width)],
                out_ref.at[:, :, pl.ds(column, width)],
                sems.at[number],
            )
        )
    for copy in copies:
        copy.start()
    for copy in copies:
        copy.wait()


def place(output, shape, pieces):
    arrays = [piece[0] for piece in pieces]
    where = tuple(piece[1:] for piece in pieces)
    aliased = output is not None
    anywhere = pl.BlockSpec(memory_space=pl.ANY)
    return pl.pallas_call(
        functools.partial(place_kernel, where, int(aliased)),
        out_shape=jax.ShapeDtypeStruct(shape, BF16),
        in_specs=[VMEM] * len(arrays) + [anywhere] * aliased,
        out_specs=anywhere,
        scratch_shapes=[pltpu.SemaphoreType.DMA((len(arrays),))],
        input_output_aliases={len(arrays): 0} if aliased else {},
        cost_estimate=pl.CostEstimate(flops=0, bytes_accessed=0, transcendentals=0),
        compiler_params=PARAMS,
    )(*arrays, *([output] if aliased else []))


def local(gradient, momentum):
    def stepped(gradient, momentum):
        return momentum_decay * momentum + gradient.astype(F32)

    ahead = gradient.astype(F32) + momentum_decay * stepped(gradient, momentum)
    experts, pairs, row_count, col_count = gradient.shape
    flat_rows = ahead.astype(BF16).reshape(experts * pairs, row_count, col_count)
    rows = lax.all_to_all(flat_rows, "tensor", split_axis=0, concat_axis=0, tiled=True)
    rows = rows.reshape(FF, col_count)

    keep, send, near, far = partial_gram(rows)
    own, to_next, to_last, to_far = chip_sum(keep, shift(send, 0, 1))
    gradient, momentum, own = lax.optimization_barrier((gradient, momentum, own))
    new_momentum = stepped(gradient, momentum)
    own, new_momentum = lax.optimization_barrier((own, new_momentum))
    mine = ring_sum(own, shift(to_next, 1), shift(to_last, -1), shift(to_far, 2))
    here = (mine, shift(mine, -1), shift(mine, 2), shift(mine, 1))
    other = shift(jnp.concatenate(here[1:]), 0, 1)
    late_rows, polys, scale = chain((*here, shift(mine, 0, 1), other), rows)

    def back(value):
        value = value.reshape(experts * pairs, row_count, value.shape[1])
        return lax.all_to_all(value, "tensor", split_axis=0, concat_axis=0, tiled=True)

    near, far, _ = lax.optimization_barrier((near, far, here[2]))
    early_rows = early_products(polys, scale, (far, shift(near, -1), shift(near, 1), shift(far, 2)))
    late = back(late_rows)
    late, early_rows = lax.optimization_barrier((late, early_rows))
    cut = late[:, :, :LATE]
    late_pieces = {0: late, 1: shift(cut, -1), 3: shift(cut, 1), 2: shift(late, 2)}
    widths = {0: FIRST, 1: LATE, 3: LATE, 2: FIRST}
    second = back(early_rows)

    shape = (experts * pairs, row_count, 8 * WIDTH)

    def late_place(pieces, steps, cross):
        return (pieces[steps], steps, cross, 0, widths[steps], 0)

    def early_places(value, cross, left, right):
        starts = {0: (0, EARLY), 1: OTHERS[0], 3: OTHERS[1], 2: OTHERS[2]}
        return [
            (value, steps, cross, WIDTH - width, width, start - left)
            for steps, (start, width) in starts.items()
            if left <= start < right
        ]

    late_across = {steps: shift(late_pieces[steps], 0, 1) for steps in (0, 1, 3)}
    places = [late_place(late_pieces, steps, 0) for steps in (0, 1, 3)]
    update = place(None, shape, places + [late_place(late_across, 0, 1)])
    late_pieces[2], update = lax.optimization_barrier((late_pieces[2], update))
    late_across[2] = shift(late_pieces[2], 0, 1)
    update = place(update, shape, [late_place(late_across, steps, 1) for steps in (1, 3)] + [late_place(late_pieces, 2, 0)])
    update = place(update, shape, [late_place(late_across, steps, 1) for steps in (2,)])
    second, update = lax.optimization_barrier((second, update))
    update = place(update, shape, early_places(second, 0, 0, SECOND))
    update = place(update, shape, early_places(shift(second, 0, 1), 1, 0, SECOND))
    return (update.reshape(experts, pairs, row_count, 8 * WIDTH), new_momentum)


def solution(mesh):
    in_specs = (P(None, None, "tensor", "replica"), P(None, None, "tensor", "replica"))
    out_specs = (P(None, None, "tensor", None), P(None, None, "tensor", "replica"))
    return jax.shard_map(local, mesh=mesh, in_specs=in_specs, out_specs=out_specs, check_vma=False)
```

```python
import functools
import math

import jax
import jax.numpy as jnp
from jax import lax
from jax.experimental import pallas as pl
from jax.experimental.pallas import tpu as pltpu
from jax.sharding import PartitionSpec as P

D = 4096
FF = 768

momentum_decay = 0.95
coef_linear = 3.4445
coef_gram = -4.775
coef_square = 2.0315
epsilon = 1e-07
scale_factor = 0.2 * math.sqrt(max(FF, D))

WIDTH = 512
LATE, MIDDLE, EARLY = 256, 0, 256
FIRST = LATE + MIDDLE
NEAR = MIDDLE + EARLY
SECOND = 2 * NEAR + 2 * EARLY
BLOCK = 256
HALF = FF
VMEM = pl.BlockSpec(memory_space=pltpu.VMEM)
HBM = pl.BlockSpec(memory_space=pltpu.HBM)
PARAMS = pltpu.CompilerParams(vmem_limit_bytes=16 * 1024 * 1024)
LARGE = pltpu.CompilerParams(vmem_limit_bytes=32 * 1024 * 1024)
F32, BF16 = jnp.float32, jnp.bfloat16


def replica_place():
    index = lax.axis_index("replica")
    return index // 2, index % 2


def shift(value, steps, cross=0):
    pairs = [
        (chip * 2 + core, ((chip + steps) % 4) * 2 + (core ^ cross))
        for chip in range(4)
        for core in range(2)
    ]
    return lax.ppermute(value, "replica", pairs)


def dot_t(left, right):
    return lax.dot_general(left, right, (((1,), (1,)), ((), ())), preferred_element_type=F32)


def dot(left, right):
    return jnp.dot(left, right, preferred_element_type=F32)


HALVES = (((0, 0), (1, 0), (1, 1)), ((2, 0), (2, 1), (2, 2)))


def gram_blocks(rows_ref, out_ref, core):
    def rows(index):
        return rows_ref[pl.ds(index * BLOCK, BLOCK), :]

    for half in range(2):

        @pl.when(core == half)
        def _():
            for place, (row, col) in enumerate(HALVES[half]):
                where = pl.ds(place * BLOCK, BLOCK)
                out_ref[where, :] = dot_t(rows(row), rows(col)).astype(out_ref.dtype)


def sent_kernel(rows_ref, send_ref):
    gram_blocks(rows_ref, send_ref, 1 - lax.axis_index("replica") % 2)


def kept_kernel(rows_ref, keep_ref, near_ref, far_ref):
    gram_blocks(rows_ref, keep_ref, lax.axis_index("replica") % 2)
    near_ref[...] = rows_ref[:, LATE:]
    far_ref[...] = rows_ref[:, FIRST:]


def sent_gram(rows):
    return pl.pallas_call(
        sent_kernel,
        out_shape=jax.ShapeDtypeStruct((HALF, BLOCK), BF16),
        in_specs=[VMEM],
        out_specs=VMEM,
        compiler_params=PARAMS,
    )(rows)


def kept_gram(rows):
    return pl.pallas_call(
        kept_kernel,
        out_shape=(
            jax.ShapeDtypeStruct((HALF, BLOCK), F32),
            jax.ShapeDtypeStruct((FF, NEAR), BF16),
            jax.ShapeDtypeStruct((FF, EARLY), BF16),
        ),
        in_specs=[VMEM],
        out_specs=(VMEM,) * 3,
        compiler_params=PARAMS,
    )(rows)


PIECE = HALF // 4


def chip_sum_kernel(keep_ref, got_ref, own_ref, next_ref, last_ref, far_ref):
    chip = lax.axis_index("replica") // 2

    def total(steps):
        where = pl.ds(pl.multiple_of(((chip + steps) % 4) * PIECE, PIECE), PIECE)
        return keep_ref[where, :] + got_ref[where, :].astype(F32)

    own_ref[...] = total(0)
    next_ref[...] = total(1).astype(BF16)
    last_ref[...] = total(3).astype(BF16)
    far_ref[...] = total(2).astype(BF16)


def chip_sum(keep, got):
    return pl.pallas_call(
        chip_sum_kernel,
        out_shape=(jax.ShapeDtypeStruct((PIECE, BLOCK), F32),)
        + (jax.ShapeDtypeStruct((PIECE, BLOCK), BF16),) * 3,
        in_specs=[VMEM, VMEM],
        out_specs=(VMEM,) * 4,
        compiler_params=PARAMS,
    )(keep, got)


def ring_sum_kernel(own_ref, a_ref, b_ref, c_ref, out_ref):
    total = own_ref[...] + a_ref[...].astype(F32) + b_ref[...].astype(F32) + c_ref[...].astype(F32)
    out_ref[...] = total.astype(BF16)


def ring_sum(own, first, second, third):
    return pl.pallas_call(
        ring_sum_kernel,
        out_shape=jax.ShapeDtypeStruct((PIECE, BLOCK), BF16),
        in_specs=[VMEM] * 4,
        out_specs=VMEM,
        compiler_params=PARAMS,
    )(own, first, second, third)


def chain_kernel(*refs):
    pieces, rows_ref = refs[:6], refs[6]
    out_ref, polys_out, scale_ref, packed, gram, polys, late, sems = refs[7:]
    index = lax.axis_index("replica")
    chip, core = index // 2, index % 2
    for steps in range(4):
        start = pl.multiple_of(((chip + steps) % 4) * PIECE, PIECE)
        packed[core, pl.ds(start, PIECE), :] = pieces[steps][...]
        if steps == 0:
            packed[1 - core, pl.ds(start, PIECE), :] = pieces[4][...]
        else:
            where = pl.ds((steps - 1) * PIECE, PIECE)
            packed[1 - core, pl.ds(start, PIECE), :] = pieces[5][where, :]
    row_id = lax.broadcasted_iota(jnp.int32, (BLOCK, BLOCK), 0)
    col_id = lax.broadcasted_iota(jnp.int32, (BLOCK, BLOCK), 1)
    diagonal = row_id == col_id
    places = ((0, 0), (1, 0), (1, 1), (2, 0), (2, 1), (2, 2))
    blocks = [packed[place // 3, pl.ds((place % 3) * BLOCK, BLOCK), :] for place in range(6)]
    squares = sum(
        jnp.sum(jnp.where(diagonal, block.astype(F32), 0.0))
        for block, (row, col) in zip(blocks, places)
        if row == col
    )
    squares = jnp.full((1, 1), squares, F32)
    scale = 1.0 / (jnp.sqrt(squares) + epsilon)
    for block, (row, col) in zip(blocks, places):
        scaled = (block.astype(F32) * scale) * scale
        gram[pl.ds(row * BLOCK, BLOCK), pl.ds(col * BLOCK, BLOCK)] = scaled.astype(BF16)
        if row != col:
            gram[pl.ds(col * BLOCK, BLOCK), pl.ds(row * BLOCK, BLOCK)] = scaled.T.astype(BF16)

    scale_ref[...] = jnp.broadcast_to(scale, scale_ref.shape)
    gram_0 = gram[...]
    poly_0 = (coef_gram * gram_0.astype(F32) + coef_square * dot(gram_0, gram_0)).astype(BF16)
    polys[0] = poly_0
    copies = [pltpu.make_async_copy(polys.at[0], polys_out.at[0], sems.at[0])]
    copies[0].start()
    rows = rows_ref[:, :FIRST]
    first = ((coef_linear * rows.astype(F32) + dot(poly_0, rows)) * scale).astype(BF16)
    half_way = (coef_linear * gram_0.astype(F32) + dot(poly_0, gram_0)).astype(BF16)
    gram_1 = (coef_linear * half_way.astype(F32) + dot(half_way, poly_0)).astype(BF16)
    for block in range(FF // BLOCK):
        where = pl.ds(block * BLOCK, BLOCK)
        cut = slice(block * BLOCK, (block + 1) * BLOCK)
        square = dot(gram_1[cut], gram_1)
        poly_1 = (coef_gram * gram_1[cut].astype(F32) + coef_square * square).astype(BF16)
        polys[1, where, :] = poly_1
        second = coef_linear * first[cut].astype(F32) + dot(poly_1, first)
        late[where, :] = (scale_factor * second).astype(BF16)
        for source, target, number in (
            (polys.at[1, where, :], polys_out.at[1, where, :], 1 + 2 * block),
            (late.at[where, :], out_ref.at[where, :], 2 + 2 * block),
        ):
            copies.append(pltpu.make_async_copy(source, target, sems.at[number]))
            copies[-1].start()
    for copy in copies:
        copy.wait()


def chain(pieces, rows):
    return pl.pallas_call(
        chain_kernel,
        out_shape=(
            jax.ShapeDtypeStruct((FF, FIRST), BF16),
            pltpu.HBM((2, FF, FF), BF16),
            jax.ShapeDtypeStruct((8, 128), F32),
        ),
        in_specs=[VMEM] * 7,
        out_specs=(HBM, HBM, VMEM),
        scratch_shapes=[
            pltpu.VMEM((2, HALF, BLOCK), BF16),
            pltpu.VMEM((FF, FF), BF16),
            pltpu.VMEM((2, FF, FF), BF16),
            pltpu.VMEM((FF, FIRST), BF16),
            pltpu.SemaphoreType.DMA((7,)),
        ],
        cost_estimate=pl.CostEstimate(flops=0, bytes_accessed=0, transcendentals=0),
        compiler_params=LARGE,
    )(*pieces, rows)


def both_steps(poly_0, poly_1, scale, rows):
    first = ((coef_linear * rows.astype(F32) + dot(poly_0, rows)) * scale).astype(BF16)
    second = coef_linear * first.astype(F32) + dot(poly_1, first)
    return (scale_factor * second).astype(BF16)


def own_kernel(polys_ref, scale_ref, early_ref, out_ref, result, sems):
    result[...] = both_steps(polys_ref[0], polys_ref[1], scale_ref[:1, :1], early_ref[...])
    store = pltpu.make_async_copy(result, out_ref.at[:, pl.ds(0, EARLY)], sems.at[0])
    store.start()
    store.wait()


ORDER = 20_000_000_000
OTHERS = ((EARLY, NEAR), (EARLY + NEAR, NEAR), (EARLY + 2 * NEAR, EARLY))


def other_kernel(polys_ref, scale_ref, *refs):
    early_in, out_ref, early, result, sems = refs[:3], *refs[4:]
    for place, (start, width) in enumerate(OTHERS):
        early[:, pl.ds(start - EARLY, width)] = early_in[place][...]
    rows = early[...]
    total = coef_linear * rows.astype(F32) + dot(polys_ref[0], rows)
    first = (total * scale_ref[:1, :1]).astype(BF16)
    stores = []
    for block in range(FF // BLOCK):
        where = pl.ds(block * BLOCK, BLOCK)
        cut = slice(block * BLOCK, (block + 1) * BLOCK)
        second = coef_linear * first[cut].astype(F32) + dot(polys_ref[1, where, :], first)
        result[where, :] = (scale_factor * second).astype(BF16)
        target = out_ref.at[where, pl.ds(EARLY, SECOND - EARLY)]
        stores.append(pltpu.make_async_copy(result.at[where, :], target, sems.at[block]))
        stores[-1].start()
    for store in stores:
        store.wait()


def early_products(polys, scale, early):
    out = jax.ShapeDtypeStruct((FF, SECOND), BF16)
    flops = 2 * FF * FF * EARLY
    result = pl.pallas_call(
        own_kernel,
        out_shape=out,
        in_specs=[VMEM] * 3,
        out_specs=HBM,
        scratch_shapes=[pltpu.VMEM((FF, EARLY), BF16), pltpu.SemaphoreType.DMA((1,))],
        cost_estimate=pl.CostEstimate(flops=0, bytes_accessed=0, transcendentals=0),
        compiler_params=PARAMS,
    )(polys, scale, early[0])
    return pl.pallas_call(
        other_kernel,
        out_shape=out,
        in_specs=[VMEM] * 5 + [HBM],
        out_specs=HBM,
        scratch_shapes=[
            pltpu.VMEM((FF, SECOND - EARLY), BF16),
            pltpu.VMEM((FF, SECOND - EARLY), BF16),
            pltpu.SemaphoreType.DMA((3,)),
        ],
        input_output_aliases={5: 0},
        cost_estimate=pl.CostEstimate(flops=ORDER, bytes_accessed=0, transcendentals=0),
        compiler_params=LARGE,
    )(polys, scale, *early[1:], result)


def place_kernel(where, aliased, *refs):
    index = lax.axis_index("replica")
    chip, core = index // 2, index % 2
    count = len(where)
    pieces, out_ref, sems = refs[:count], refs[count + aliased], refs[count + aliased + 1]
    copies = []
    for number, (steps, cross, first, width, source) in enumerate(where):
        block = ((chip + steps) % 4) * 2 + (1 - core if cross else core)
        column = pl.multiple_of(block * WIDTH + first, 128)
        copies.append(
            pltpu.make_async_copy(
                pieces[number].at[:, :, pl.ds(source, width)],
                out_ref.at[:, :, pl.ds(column, width)],
                sems.at[number],
            )
        )
    for copy in copies:
        copy.start()
    for copy in copies:
        copy.wait()


def place(output, shape, pieces):
    arrays = [piece[0] for piece in pieces]
    where = tuple(piece[1:] for piece in pieces)
    aliased = output is not None
    anywhere = pl.BlockSpec(memory_space=pl.ANY)
    return pl.pallas_call(
        functools.partial(place_kernel, where, int(aliased)),
        out_shape=jax.ShapeDtypeStruct(shape, BF16),
        in_specs=[VMEM] * len(arrays) + [anywhere] * aliased,
        out_specs=anywhere,
        scratch_shapes=[pltpu.SemaphoreType.DMA((len(arrays),))],
        input_output_aliases={len(arrays): 0} if aliased else {},
        cost_estimate=pl.CostEstimate(flops=0, bytes_accessed=0, transcendentals=0),
        compiler_params=PARAMS,
    )(*arrays, *([output] if aliased else []))


def local(gradient, momentum):
    def stepped(gradient, momentum):
        return momentum_decay * momentum + gradient.astype(F32)

    ahead = gradient.astype(F32) + momentum_decay * stepped(gradient, momentum)
    experts, pairs, row_count, col_count = gradient.shape
    flat_rows = ahead.astype(BF16).reshape(experts * pairs, row_count, col_count)
    rows = lax.all_to_all(flat_rows, "tensor", split_axis=0, concat_axis=0, tiled=True)
    rows = rows.reshape(FF, col_count)

    send = sent_gram(rows)
    keep, near, far = kept_gram(rows)
    own, to_next, to_last, to_far = chip_sum(keep, shift(send, 0, 1))
    gradient, momentum, own = lax.optimization_barrier((gradient, momentum, own))
    new_momentum = stepped(gradient, momentum)
    own, new_momentum = lax.optimization_barrier((own, new_momentum))
    mine = ring_sum(own, shift(to_next, 1), shift(to_last, -1), shift(to_far, 2))
    here = (mine, shift(mine, -1), shift(mine, 2), shift(mine, 1))
    other = shift(jnp.concatenate(here[1:]), 0, 1)
    late_rows, polys, scale = chain((*here, shift(mine, 0, 1), other), rows)

    def back(value):
        value = value.reshape(experts * pairs, row_count, value.shape[1])
        return lax.all_to_all(value, "tensor", split_axis=0, concat_axis=0, tiled=True)

    near, far, _ = lax.optimization_barrier((near, far, here[2]))
    early_rows = early_products(polys, scale, (far, shift(near, -1), shift(near, 1), shift(far, 2)))
    late = back(late_rows)
    late, early_rows = lax.optimization_barrier((late, early_rows))
    cut = late[:, :, :LATE]
    late_pieces = {0: late, 1: shift(cut, -1), 3: shift(cut, 1), 2: shift(late, 2)}
    widths = {0: FIRST, 1: LATE, 3: LATE, 2: FIRST}
    second = back(early_rows)

    shape = (experts * pairs, row_count, 8 * WIDTH)

    def late_place(pieces, steps, cross):
        return (pieces[steps], steps, cross, 0, widths[steps], 0)

    def early_places(value, cross, left, right):
        starts = {0: (0, EARLY), 1: OTHERS[0], 3: OTHERS[1], 2: OTHERS[2]}
        return [
            (value, steps, cross, WIDTH - width, width, start - left)
            for steps, (start, width) in starts.items()
            if left <= start < right
        ]

    late_across = {steps: shift(late_pieces[steps], 0, 1) for steps in (0, 1, 3)}
    places = [late_place(late_pieces, steps, 0) for steps in (0, 1, 3)]
    update = place(None, shape, places + [late_place(late_across, 0, 1)])
    late_pieces[2], update = lax.optimization_barrier((late_pieces[2], update))
    late_across[2] = shift(late_pieces[2], 0, 1)
    update = place(update, shape, [late_place(late_across, steps, 1) for steps in (1, 3)] + [late_place(late_pieces, 2, 0)])
    update = place(update, shape, [late_place(late_across, steps, 1) for steps in (2,)])
    second, update = lax.optimization_barrier((second, update))
    update = place(update, shape, early_places(second, 0, 0, SECOND))
    middle = EARLY + NEAR
    for left, right in ((0, middle), (middle, SECOND)):
        across = shift(second[:, :, left:right], 0, 1)
        update = place(update, shape, early_places(across, 1, left, right))
    return (update.reshape(experts, pairs, row_count, 8 * WIDTH), new_momentum)


def solution(mesh):
    in_specs = (P(None, None, "tensor", "replica"), P(None, None, "tensor", "replica"))
    out_specs = (P(None, None, "tensor", None), P(None, None, "tensor", "replica"))
    return jax.shard_map(local, mesh=mesh, in_specs=in_specs, out_specs=out_specs, check_vma=False)
```

```python
import functools
import math

import jax
import jax.numpy as jnp
from jax import lax
from jax.experimental import pallas as pl
from jax.experimental.pallas import tpu as pltpu
from jax.sharding import PartitionSpec as P

D = 4096
FF = 768

momentum_decay = 0.95
coef_linear = 3.4445
coef_gram = -4.775
coef_square = 2.0315
epsilon = 1e-07
scale_factor = 0.2 * math.sqrt(max(FF, D))

WIDTH = 512
LATE, MIDDLE, EARLY = 256, 0, 256
FIRST = LATE + MIDDLE
NEAR = MIDDLE + EARLY
SECOND = 2 * NEAR + 2 * EARLY
BLOCK = 256
HALF = FF
VMEM = pl.BlockSpec(memory_space=pltpu.VMEM)
HBM = pl.BlockSpec(memory_space=pltpu.HBM)
PARAMS = pltpu.CompilerParams(vmem_limit_bytes=16 * 1024 * 1024)
LARGE = pltpu.CompilerParams(vmem_limit_bytes=32 * 1024 * 1024)
F32, BF16 = jnp.float32, jnp.bfloat16


def replica_place():
    index = lax.axis_index("replica")
    return index // 2, index % 2


def shift(value, steps, cross=0):
    pairs = [
        (chip * 2 + core, ((chip + steps) % 4) * 2 + (core ^ cross))
        for chip in range(4)
        for core in range(2)
    ]
    return lax.ppermute(value, "replica", pairs)


def dot_t(left, right):
    return lax.dot_general(left, right, (((1,), (1,)), ((), ())), preferred_element_type=F32)


def dot(left, right):
    return jnp.dot(left, right, preferred_element_type=F32)


HALVES = (((0, 0), (1, 0), (1, 1)), ((2, 0), (2, 1), (2, 2)))


def gram_blocks(rows_ref, out_ref, core):
    def rows(index):
        return rows_ref[pl.ds(index * BLOCK, BLOCK), :]

    for half in range(2):

        @pl.when(core == half)
        def _():
            for place, (row, col) in enumerate(HALVES[half]):
                where = pl.ds(place * BLOCK, BLOCK)
                out_ref[where, :] = dot_t(rows(row), rows(col)).astype(out_ref.dtype)


def sent_kernel(rows_ref, send_ref):
    gram_blocks(rows_ref, send_ref, 1 - lax.axis_index("replica") % 2)


def kept_kernel(rows_ref, keep_ref, near_ref, far_ref):
    gram_blocks(rows_ref, keep_ref, lax.axis_index("replica") % 2)
    near_ref[...] = rows_ref[:, LATE:]
    far_ref[...] = rows_ref[:, FIRST:]


def sent_gram(rows):
    return pl.pallas_call(
        sent_kernel,
        out_shape=jax.ShapeDtypeStruct((HALF, BLOCK), BF16),
        in_specs=[VMEM],
        out_specs=VMEM,
        compiler_params=PARAMS,
    )(rows)


def kept_gram(rows):
    return pl.pallas_call(
        kept_kernel,
        out_shape=(
            jax.ShapeDtypeStruct((HALF, BLOCK), F32),
            jax.ShapeDtypeStruct((FF, NEAR), BF16),
            jax.ShapeDtypeStruct((FF, EARLY), BF16),
        ),
        in_specs=[VMEM],
        out_specs=(VMEM,) * 3,
        compiler_params=PARAMS,
    )(rows)


PIECE = HALF // 4


def chip_sum_kernel(keep_ref, got_ref, own_ref, next_ref, last_ref, far_ref):
    chip = lax.axis_index("replica") // 2

    def total(steps):
        where = pl.ds(pl.multiple_of(((chip + steps) % 4) * PIECE, PIECE), PIECE)
        return keep_ref[where, :] + got_ref[where, :].astype(F32)

    own_ref[...] = total(0)
    next_ref[...] = total(1).astype(BF16)
    last_ref[...] = total(3).astype(BF16)
    far_ref[...] = total(2).astype(BF16)


def chip_sum(keep, got):
    return pl.pallas_call(
        chip_sum_kernel,
        out_shape=(jax.ShapeDtypeStruct((PIECE, BLOCK), F32),)
        + (jax.ShapeDtypeStruct((PIECE, BLOCK), BF16),) * 3,
        in_specs=[VMEM, VMEM],
        out_specs=(VMEM,) * 4,
        compiler_params=PARAMS,
    )(keep, got)


def ring_sum_kernel(own_ref, a_ref, b_ref, c_ref, out_ref):
    total = own_ref[...] + a_ref[...].astype(F32) + b_ref[...].astype(F32) + c_ref[...].astype(F32)
    out_ref[...] = total.astype(BF16)


def ring_sum(own, first, second, third):
    return pl.pallas_call(
        ring_sum_kernel,
        out_shape=jax.ShapeDtypeStruct((PIECE, BLOCK), BF16),
        in_specs=[VMEM] * 4,
        out_specs=VMEM,
        compiler_params=PARAMS,
    )(own, first, second, third)


def chain_kernel(*refs):
    pieces, rows_ref = refs[:6], refs[6]
    out_ref, polys_out, scale_ref, packed, gram, polys, late, sems = refs[7:]
    index = lax.axis_index("replica")
    chip, core = index // 2, index % 2
    for steps in range(4):
        start = pl.multiple_of(((chip + steps) % 4) * PIECE, PIECE)
        packed[core, pl.ds(start, PIECE), :] = pieces[steps][...]
        if steps == 0:
            packed[1 - core, pl.ds(start, PIECE), :] = pieces[4][...]
        else:
            where = pl.ds((steps - 1) * PIECE, PIECE)
            packed[1 - core, pl.ds(start, PIECE), :] = pieces[5][where, :]
    row_id = lax.broadcasted_iota(jnp.int32, (BLOCK, BLOCK), 0)
    col_id = lax.broadcasted_iota(jnp.int32, (BLOCK, BLOCK), 1)
    diagonal = row_id == col_id
    places = ((0, 0), (1, 0), (1, 1), (2, 0), (2, 1), (2, 2))
    blocks = [packed[place // 3, pl.ds((place % 3) * BLOCK, BLOCK), :] for place in range(6)]
    for block, (row, col) in zip(blocks, places):
        gram[pl.ds(row * BLOCK, BLOCK), pl.ds(col * BLOCK, BLOCK)] = block
        if row != col:
            flipped = block.astype(F32).T.astype(BF16)
            gram[pl.ds(col * BLOCK, BLOCK), pl.ds(row * BLOCK, BLOCK)] = flipped
    squares = sum(
        jnp.sum(jnp.where(diagonal, block.astype(F32), 0.0))
        for block, (row, col) in zip(blocks, places)
        if row == col
    )
    scale = 1.0 / (jnp.sqrt(jnp.full((1, 1), squares, F32)) + epsilon)
    scale_ref[...] = jnp.broadcast_to(scale, scale_ref.shape)
    second_power = scale * scale
    fourth_power = second_power * second_power
    raw = gram[...]
    poly_0 = (coef_gram * second_power) * raw.astype(F32)
    poly_0 = (poly_0 + (coef_square * fourth_power) * dot(raw, raw)).astype(BF16)
    polys[0] = poly_0
    copies = [pltpu.make_async_copy(polys.at[0], polys_out.at[0], sems.at[0])]
    copies[0].start()
    rows = rows_ref[:, :FIRST]
    first = ((coef_linear * rows.astype(F32) + dot(poly_0, rows)) * scale).astype(BF16)
    half_way = coef_linear * raw.astype(F32) + dot(poly_0, raw)
    half_way = (second_power * half_way).astype(BF16)
    gram_1 = (coef_linear * half_way.astype(F32) + dot(half_way, poly_0)).astype(BF16)
    for block in range(FF // BLOCK):
        where = pl.ds(block * BLOCK, BLOCK)
        cut = slice(block * BLOCK, (block + 1) * BLOCK)
        square = dot(gram_1[cut], gram_1)
        poly_1 = (coef_gram * gram_1[cut].astype(F32) + coef_square * square).astype(BF16)
        polys[1, where, :] = poly_1
        second = coef_linear * first[cut].astype(F32) + dot(poly_1, first)
        late[where, :] = (scale_factor * second).astype(BF16)
        for source, target, number in (
            (polys.at[1, where, :], polys_out.at[1, where, :], 1 + 2 * block),
            (late.at[where, :], out_ref.at[where, :], 2 + 2 * block),
        ):
            copies.append(pltpu.make_async_copy(source, target, sems.at[number]))
            copies[-1].start()
    for copy in copies:
        copy.wait()


def chain(pieces, rows):
    return pl.pallas_call(
        chain_kernel,
        out_shape=(
            jax.ShapeDtypeStruct((FF, FIRST), BF16),
            pltpu.HBM((2, FF, FF), BF16),
            jax.ShapeDtypeStruct((8, 128), F32),
        ),
        in_specs=[VMEM] * 7,
        out_specs=(HBM, HBM, VMEM),
        scratch_shapes=[
            pltpu.VMEM((2, HALF, BLOCK), BF16),
            pltpu.VMEM((FF, FF), BF16),
            pltpu.VMEM((2, FF, FF), BF16),
            pltpu.VMEM((FF, FIRST), BF16),
            pltpu.SemaphoreType.DMA((7,)),
        ],
        cost_estimate=pl.CostEstimate(flops=0, bytes_accessed=0, transcendentals=0),
        compiler_params=LARGE,
    )(*pieces, rows)


def both_steps(poly_0, poly_1, scale, rows):
    first = ((coef_linear * rows.astype(F32) + dot(poly_0, rows)) * scale).astype(BF16)
    second = coef_linear * first.astype(F32) + dot(poly_1, first)
    return (scale_factor * second).astype(BF16)


def own_kernel(polys_ref, scale_ref, early_ref, out_ref, result, sems):
    result[...] = both_steps(polys_ref[0], polys_ref[1], scale_ref[:1, :1], early_ref[...])
    store = pltpu.make_async_copy(result, out_ref.at[:, pl.ds(0, EARLY)], sems.at[0])
    store.start()
    store.wait()


ORDER = 20_000_000_000
OTHERS = ((EARLY, NEAR), (EARLY + NEAR, NEAR), (EARLY + 2 * NEAR, EARLY))


def other_kernel(polys_ref, scale_ref, *refs):
    early_in, out_ref, early, result, sems = refs[:3], *refs[4:]
    for place, (start, width) in enumerate(OTHERS):
        early[:, pl.ds(start - EARLY, width)] = early_in[place][...]
    rows = early[...]
    total = coef_linear * rows.astype(F32) + dot(polys_ref[0], rows)
    first = (total * scale_ref[:1, :1]).astype(BF16)
    stores = []
    for block in range(FF // BLOCK):
        where = pl.ds(block * BLOCK, BLOCK)
        cut = slice(block * BLOCK, (block + 1) * BLOCK)
        second = coef_linear * first[cut].astype(F32) + dot(polys_ref[1, where, :], first)
        result[where, :] = (scale_factor * second).astype(BF16)
        target = out_ref.at[where, pl.ds(EARLY, SECOND - EARLY)]
        stores.append(pltpu.make_async_copy(result.at[where, :], target, sems.at[block]))
        stores[-1].start()
    for store in stores:
        store.wait()


def early_products(polys, scale, early):
    out = jax.ShapeDtypeStruct((FF, SECOND), BF16)
    flops = 2 * FF * FF * EARLY
    result = pl.pallas_call(
        own_kernel,
        out_shape=out,
        in_specs=[VMEM] * 3,
        out_specs=HBM,
        scratch_shapes=[pltpu.VMEM((FF, EARLY), BF16), pltpu.SemaphoreType.DMA((1,))],
        cost_estimate=pl.CostEstimate(flops=0, bytes_accessed=0, transcendentals=0),
        compiler_params=PARAMS,
    )(polys, scale, early[0])
    return pl.pallas_call(
        other_kernel,
        out_shape=out,
        in_specs=[VMEM] * 5 + [HBM],
        out_specs=HBM,
        scratch_shapes=[
            pltpu.VMEM((FF, SECOND - EARLY), BF16),
            pltpu.VMEM((FF, SECOND - EARLY), BF16),
            pltpu.SemaphoreType.DMA((3,)),
        ],
        input_output_aliases={5: 0},
        cost_estimate=pl.CostEstimate(flops=ORDER, bytes_accessed=0, transcendentals=0),
        compiler_params=LARGE,
    )(polys, scale, *early[1:], result)


def place_kernel(where, aliased, *refs):
    index = lax.axis_index("replica")
    chip, core = index // 2, index % 2
    count = len(where)
    pieces, out_ref, sems = refs[:count], refs[count + aliased], refs[count + aliased + 1]
    copies = []
    for number, (steps, cross, first, width, source) in enumerate(where):
        block = ((chip + steps) % 4) * 2 + (1 - core if cross else core)
        column = pl.multiple_of(block * WIDTH + first, 128)
        copies.append(
            pltpu.make_async_copy(
                pieces[number].at[:, :, pl.ds(source, width)],
                out_ref.at[:, :, pl.ds(column, width)],
                sems.at[number],
            )
        )
    for copy in copies:
        copy.start()
    for copy in copies:
        copy.wait()


def place(output, shape, pieces):
    arrays = [piece[0] for piece in pieces]
    where = tuple(piece[1:] for piece in pieces)
    aliased = output is not None
    anywhere = pl.BlockSpec(memory_space=pl.ANY)
    return pl.pallas_call(
        functools.partial(place_kernel, where, int(aliased)),
        out_shape=jax.ShapeDtypeStruct(shape, BF16),
        in_specs=[VMEM] * len(arrays) + [anywhere] * aliased,
        out_specs=anywhere,
        scratch_shapes=[pltpu.SemaphoreType.DMA((len(arrays),))],
        input_output_aliases={len(arrays): 0} if aliased else {},
        cost_estimate=pl.CostEstimate(flops=0, bytes_accessed=0, transcendentals=0),
        compiler_params=PARAMS,
    )(*arrays, *([output] if aliased else []))


def local(gradient, momentum):
    def stepped(gradient, momentum):
        return momentum_decay * momentum + gradient.astype(F32)

    ahead = gradient.astype(F32) + momentum_decay * stepped(gradient, momentum)
    experts, pairs, row_count, col_count = gradient.shape
    flat_rows = ahead.astype(BF16).reshape(experts * pairs, row_count, col_count)
    rows = lax.all_to_all(flat_rows, "tensor", split_axis=0, concat_axis=0, tiled=True)
    rows = rows.reshape(FF, col_count)

    send = sent_gram(rows)
    keep, near, far = kept_gram(rows)
    own, to_next, to_last, to_far = chip_sum(keep, shift(send, 0, 1))
    gradient, momentum, own = lax.optimization_barrier((gradient, momentum, own))
    new_momentum = stepped(gradient, momentum)
    own, new_momentum = lax.optimization_barrier((own, new_momentum))
    mine = ring_sum(own, shift(to_next, 1), shift(to_last, -1), shift(to_far, 2))
    here = (mine, shift(mine, -1), shift(mine, 2), shift(mine, 1))
    other = shift(jnp.concatenate(here[1:]), 0, 1)
    late_rows, polys, scale = chain((*here, shift(mine, 0, 1), other), rows)

    def back(value):
        value = value.reshape(experts * pairs, row_count, value.shape[1])
        return lax.all_to_all(value, "tensor", split_axis=0, concat_axis=0, tiled=True)

    near, far, _ = lax.optimization_barrier((near, far, here[2]))
    early_rows = early_products(polys, scale, (far, shift(near, -1), shift(near, 1), shift(far, 2)))
    late = back(late_rows)
    late, early_rows = lax.optimization_barrier((late, early_rows))
    cut = late[:, :, :LATE]
    late_pieces = {0: late, 1: shift(cut, -1), 3: shift(cut, 1), 2: shift(late, 2)}
    widths = {0: FIRST, 1: LATE, 3: LATE, 2: FIRST}
    second = back(early_rows)

    shape = (experts * pairs, row_count, 8 * WIDTH)

    def late_place(pieces, steps, cross):
        return (pieces[steps], steps, cross, 0, widths[steps], 0)

    def early_places(value, cross, left, right):
        starts = {0: (0, EARLY), 1: OTHERS[0], 3: OTHERS[1], 2: OTHERS[2]}
        return [
            (value, steps, cross, WIDTH - width, width, start - left)
            for steps, (start, width) in starts.items()
            if left <= start < right
        ]

    late_across = {steps: shift(late_pieces[steps], 0, 1) for steps in (0, 1, 3)}
    places = [late_place(late_pieces, steps, 0) for steps in (0, 1, 3)]
    update = place(None, shape, places + [late_place(late_across, 0, 1)])
    late_pieces[2], update = lax.optimization_barrier((late_pieces[2], update))
    late_across[2] = shift(late_pieces[2], 0, 1)
    update = place(update, shape, [late_place(late_across, steps, 1) for steps in (1, 3)] + [late_place(late_pieces, 2, 0)])
    update = place(update, shape, [late_place(late_across, steps, 1) for steps in (2,)])
    second, update = lax.optimization_barrier((second, update))
    update = place(update, shape, early_places(second, 0, 0, SECOND))
    middle = EARLY + NEAR
    for left, right in ((0, middle), (middle, SECOND)):
        across = shift(second[:, :, left:right], 0, 1)
        update = place(update, shape, early_places(across, 1, left, right))
    return (update.reshape(experts, pairs, row_count, 8 * WIDTH), new_momentum)


def solution(mesh):
    in_specs = (P(None, None, "tensor", "replica"), P(None, None, "tensor", "replica"))
    out_specs = (P(None, None, "tensor", None), P(None, None, "tensor", "replica"))
    return jax.shard_map(local, mesh=mesh, in_specs=in_specs, out_specs=out_specs, check_vma=False)
```
